128 devices in a mesh: dp: 4 (over z_lo, core), row: 8 (over z_hi, x), col: 4 (over y).
Axes of the slice: x: 4, y: 4, z: 4 (z_hi: 2, z_lo: 2; z = z_hi * 2 + z_lo), core: 2. Of those that a mesh axis runs over, the one named last changes fastest.
Arguments:
- block_input: bfloat16 [16384, 1536], P(('dp', 'col'), 'row'), may hold values from -6 to 6
- attn_gain: bfloat16 [1536], P('row'), may hold values from 0.5 to 1.5
- attn_weight: bfloat16 [1536, 4, 1536], P('row', None, 'col'), may hold values from -0.15625 to 0.15625
- forget_weight: bfloat16 [1536, 24], P('row', 'col'), may hold values from -0.15625 to 0.15625
- forget_bias: float32 [24], P('col'), may hold values from 2 to 8
- out_weight: bfloat16 [1536, 1536], P('col', 'row'), may hold values from -1.25 to 1.25
- ffn_gain: bfloat16 [1536], P('row'), may hold values from 0.5 to 1.5
- gate_up_weight: bfloat16 [1536, 2, 4096], P('row', None, 'col'), may hold values from -0.15625 to 0.15625
- down_weight: bfloat16 [4096, 1536], P('col', 'row'), may hold values from -0.09375 to 0.09375
- segments: int32 [8, 2048], P('dp'), may hold values from 0 to 3, never falling along the last dimension, each value on 1 to 1280 neighbouring positions
- cotangent: bfloat16 [16384, 1536], P(('dp', 'col'), 'row'), may hold values from -6 to 6
Outputs:
- block_output: bfloat16 [16384, 1536], P(('dp', 'col'), 'row')
- input_grad: float32 [16384, 1536], P(('dp', 'col'), 'row')
- attn_gain_grad: float32 [1536], P('row')
- attn_weight_grad: float32 [1536, 4, 1536], P('row', None, 'col')
- forget_weight_grad: float32 [1536, 24], P('row', 'col')
- forget_bias_grad: float32 [24], P('col')
- out_weight_grad: float32 [1536, 1536], P('col', 'row')
- ffn_gain_grad: float32 [1536], P('row')
- gate_up_weight_grad: float32 [1536, 2, 4096], P('row', None, 'col')
- down_weight_grad: float32 [4096, 1536], P('col', 'row')
The draws below stay inside these ranges and needn't reach their ends.
Inputs may be any that keep to these rules, and one draw needn't show every extreme that they name: `segments`: in each sequence the document numbers start at 0 and never fall; every one of the 4 numbers occurs, and one document holds exactly 1280 tokens.
All inputs are finite; a program needn't handle non-finite values.
Results may differ from the reference program's by a relative error of at most 0.017.
The reference program's roundings to bfloat16 on the way count: a program that leaves them out, or rounds other values in their place, can miss the bound.
Values may be sent and summed in bfloat16 or wider, within the bound.
No kernel may reach another device: no remote copies, remote signals or barrier semaphores. Data moves between devices by JAX's collectives and lax.ppermute only.
A program may use at most 256 MiB of HBM per device.

```python
import math
import jax
import jax.numpy as jnp
import numpy as np
from jax import lax

D = 1536
HEADS = 24
HEAD_DIM = 64
FF = 4096
WINDOW = 1024
LENGTH = 2048
SEQS = 8
TOKENS = 16384


def steps_of(key, dims, shards, least, top_value):
    def one(axis_at, parts):
        heights = jax.random.uniform(jax.random.fold_in(jax.random.fold_in(key, 6), axis_at), (parts,), jnp.float32, least / len(shards), top_value / len(shards))
        return jnp.repeat(jnp.exp(heights), dims[axis_at] // parts).reshape((-1,) + (1,) * (len(dims) - axis_at - 1))

    level = one(*shards[0])
    for cut in shards[1:]:
        level = level * one(*cut)
    return level


def length_profile(amount, total, bound, slope):
    portions = [(1 << 20) // math.isqrt(grade ** slope) + 1 for grade in range(2, amount + 1)]
    rest, holding = total - bound - (amount - 1), [1] * (amount - 1)
    while rest > 0:
        candidates = [i for i in range(amount - 1) if holding[i] < bound]
        mass, remaining = sum([portions[i] for i in candidates]), rest
        for i in candidates:
            extra = min(bound - holding[i], max(1, remaining * portions[i] // mass), rest)
            holding[i] = holding[i] + extra
            rest = rest - extra
    return np.array([bound] + holding)


def ragged_sizes(key, count, total, most, slope):
    if count == 2:
        one = jax.random.randint(key, (), max(1, total - most), min(most, total - 1) + 1)
        return jnp.stack([one, total - one])
    lengths = jnp.asarray(length_profile(count, total, most, slope), jnp.int32)
    pairs = (count - 1) // 2
    giver, receiver = lengths[1:1 + 2 * pairs:2], lengths[2:2 + 2 * pairs:2]
    margin = jnp.minimum(giver - 1, most - receiver)
    moved = jax.random.randint(jax.random.fold_in(key, 1), (pairs,), 0, 1 << 20) % (margin + 1)
    lengths = lengths.at[1:1 + 2 * pairs:2].set(giver - moved).at[2:2 + 2 * pairs:2].set(receiver + moved)
    return lengths[jax.random.permutation(jax.random.fold_in(key, 2), count)]


def centred(own_key, dims, deviation, bound, cuts=(), kind=jnp.bfloat16):
    array = deviation * jax.random.normal(own_key, dims, jnp.float32)
    if cuts:
        array = array * steps_of(own_key, dims, cuts, -0.22, 0.18)
    return jnp.clip(array, -bound, bound).astype(kind)


def setup_inputs(seed: int = 0) -> dict:
    seeds = jax.random.split(jax.random.key(seed), 12)
    return {
        "block_input": centred(seeds[0], (TOKENS, D), 1.0, 6.0, ((0, 16), (1, 8))),
        "attn_gain": jnp.clip(1.0 + 0.1 * jax.random.normal(seeds[1], (D,), jnp.float32), 0.5, 1.5).astype(jnp.bfloat16),
        "attn_weight": centred(seeds[2], (D, 4, D), D ** -0.5, 0.15625, ((0, 8), (2, 4))),
        "forget_weight": centred(seeds[3], (D, HEADS), D ** -0.5, 0.15625, ((0, 8), (1, 4))),
        "forget_bias": jnp.clip(2.0 + 6.0 * jax.random.uniform(seeds[4], (HEADS,), jnp.float32) ** steps_of(seeds[4], (HEADS,), ((0, 4),), -0.2, 0.2), 2.0, 8.0),
        "out_weight": centred(seeds[5], (D, D), (D // 64) ** -0.5, 1.25, ((0, 4), (1, 8))),
        "ffn_gain": jnp.clip(1.0 + 0.1 * jax.random.normal(seeds[6], (D,), jnp.float32), 0.5, 1.5).astype(jnp.bfloat16),
        "gate_up_weight": centred(seeds[7], (D, 2, FF), D ** -0.5, 0.15625, ((0, 8), (2, 4))),
        "down_weight": centred(seeds[8], (FF, D), FF ** -0.5, 0.09375, ((0, 4), (1, 8))),
        "segments": jax.vmap(lambda own: jnp.searchsorted(jnp.cumsum(ragged_sizes(own, 4, LENGTH, 5 * LENGTH // 8, 0)), jnp.arange(LENGTH), side="right"))(jax.random.split(seeds[9], SEQS)).reshape((SEQS, LENGTH)).astype(jnp.int32),
        "cotangent": centred(seeds[10], (TOKENS, D), 1.0, 6.0, ((0, 16), (1, 8))),
    }


epsilon = 1e-06
masked_score = -1e+30
highest = lax.Precision.HIGHEST

@jax.custom_vjp
def low(v):
    return lax.optimization_barrier(v.astype(jnp.bfloat16)).astype(jnp.float32)

@jax.custom_vjp
def low_back(v):
    return v

def low_keep(v):
    return (low(v), None)

def low_pass(kept, grad):
    return (grad,)

def back_keep(v):
    return (v, None)

def back_low(kept, grad):
    return (low(grad),)
low.defvjp(low_keep, low_pass)
low_back.defvjp(back_keep, back_low)

def product(left_side, right_side):
    return jnp.dot(left_side, right_side, precision=highest)

def norm_rows(values, gain_values):
    return values * lax.rsqrt(lax.optimization_barrier(jnp.mean(values * values, axis=-1, keepdims=True)) + epsilon) * gain_values

def attend_one(query_rows, key_rows, value_rows, cumulative, segment):
    scores = product(query_rows, key_rows.T) * HEAD_DIM ** (-0.5) + cumulative[:, None] - cumulative[None, :]
    scores = low_back(scores)
    positions = jnp.arange(LENGTH, dtype=jnp.int32)
    token_gap = positions[:, None] - positions[None, :]
    allowed = (token_gap >= 0) & (token_gap < WINDOW) & (segment[:, None] == segment[None, :])
    softmax_weights = low(jax.nn.softmax(jnp.where(allowed, scores, masked_score), axis=-1))
    return product(softmax_weights, value_rows)

def attend_item(pieces):
    return jax.checkpoint(attend_one)(pieces[0], pieces[1], pieces[2], pieces[3], pieces[4])

def layer(block_input, attn_gain, attn_weight, forget_weight, forget_bias, out_weight, ffn_gain, gate_up_weight, down_weight, segments):
    seq_count = segments.shape[0]
    normed = low(norm_rows(block_input, attn_gain))
    projected = product(normed, attn_weight.reshape(D, 4 * D))
    query_rows = low(low_back(projected[:, :D]))
    key_rows = low(low_back(projected[:, D:2 * D]))
    value_rows = low(low_back(projected[:, 2 * D:3 * D]))
    gate_logit = low_back(projected[:, 3 * D:])
    forget_logit = product(normed, forget_weight) + forget_bias
    cumulative = jnp.cumsum(jax.nn.log_sigmoid(forget_logit).reshape(seq_count, LENGTH, HEADS), axis=1)

    def by_head(matrix):
        return matrix.reshape(seq_count, LENGTH, HEADS, HEAD_DIM).transpose(0, 2, 1, 3).reshape(seq_count * HEADS, LENGTH, HEAD_DIM)
    per_head = (by_head(query_rows), by_head(key_rows), by_head(value_rows), cumulative.transpose(0, 2, 1).reshape(seq_count * HEADS, LENGTH), jnp.repeat(segments, HEADS, axis=0))
    attended = lax.map(attend_item, per_head)
    attended = attended.reshape(seq_count, HEADS, LENGTH, HEAD_DIM).transpose(0, 2, 1, 3).reshape(seq_count * LENGTH, D)
    attended = low_back(attended)
    gated = low(attended * jax.nn.sigmoid(gate_logit))
    residual = block_input + low_back(product(gated, out_weight))
    normed_second = low(norm_rows(residual, ffn_gain))
    both_halves = product(normed_second, gate_up_weight.reshape(D, 2 * FF))
    gate_rows = low_back(both_halves[:, :FF])
    up_rows = low_back(both_halves[:, FF:])
    hidden = low(jax.nn.silu(gate_rows) * up_rows)
    return residual + low_back(product(hidden, down_weight))

def reference(block_input, attn_gain, attn_weight, forget_weight, forget_bias, out_weight, ffn_gain, gate_up_weight, down_weight, segments, cotangent):
    floats = tuple((argument.astype(jnp.float32) for argument in (block_input, attn_gain, attn_weight, forget_weight, forget_bias, out_weight, ffn_gain, gate_up_weight, down_weight)))

    def forward(*arrays):
        return layer(*arrays, segments)
    output, pullback = jax.vjp(forward, *floats)
    gradients = pullback(cotangent.astype(jnp.float32))
    return (output.astype(jnp.bfloat16), gradients[0], gradients[1], gradients[2], gradients[3], gradients[4], gradients[5], gradients[6], gradients[7], gradients[8])
```

```python
import jax
import jax.numpy as jnp
from jax import lax
from jax.experimental import pallas as pl
from jax.experimental.layout import Layout, with_layout_constraint
from jax.experimental.pallas import tpu as pltpu
from jax.sharding import Mesh, PartitionSpec as P

D = 1536
HEAD_DIM = 64
WINDOW = 1024
EPS = 1e-06
MASKED = -1e30
ALL = ("zl", "core", "zh", "x", "y")
DIMS = (2, 2, 2, 4, 4)
BF = jnp.bfloat16
F32 = jnp.float32
HIGHEST = lax.Precision.HIGHEST

TB = 512
KW = 3 * TB
CH = 128
SPAN = WINDOW + CH
GROUP_COLS = 4
EXT = 128
HEADS_COL = 6
PIECES = 4
SHARD = D // 8
WIDE = 2 * SHARD
QUARTER = TB // GROUP_COLS
ROWS_IN = TB + QUARTER + 16
ROWS_OUT = TB + QUARTER
TILE = 256


def place(zl, core, zh, x, y):
    return (((zl * 2 + core) * 2 + zh) * 4 + x) * 4 + y


def places():
    for zl in range(2):
        for core in range(2):
            for zh in range(2):
                for x in range(4):
                    for y in range(4):
                        yield zl, core, zh, x, y


def to_groups(step):
    return [
        (
            place(zl, core, zh, x, y),
            place(zl, y % 2, y // 2, 2 * core + x % 2, (2 * zh + x // 2) ^ step),
        )
        for zl, core, zh, x, y in places()
    ]


def from_groups(step):
    return [(target, source) for source, target in to_groups(step)]


def flip(value, axis, size, bits):
    return lax.ppermute(value, axis, [(i, i ^ bits) for i in range(size)])


def core_flip(value):
    return flip(value, "core", 2, 1)


def z_partner(value):
    return flip(value, ("zl", "zh"), 4, 3)


def zh_flip(value):
    return flip(value, "zh", 2, 1)


def z_twin(value):
    return flip(value, "zl", 2, 1)


def x_flip(value, bits):
    return flip(value, "x", 4, bits)


def y_flip(value, bits):
    return flip(value, "y", 4, bits)


def block_shift(value, distance):
    pairs = []
    for core in range(2):
        for x in range(4):
            block = 2 * core + x % 2
            other = block + distance
            if 0 <= other < 4:
                pairs.append((core * 4 + x, (other // 2) * 4 + (x // 2) * 2 + other % 2))
    return lax.ppermute(value, ("core", "x"), pairs)


def dot(a, b):
    return lax.dot_general(a, b, (((1,), (0,)), ((), ())), preferred_element_type=F32)


def dot_t(a, b):
    return lax.dot_general(a, b, (((1,), (1,)), ((), ())), preferred_element_type=F32)


def t_dot(a, b):
    return lax.dot_general(a, b, (((0,), (0,)), ((), ())), preferred_element_type=F32)


def rounded(value):
    return lax.reduce_precision(value, exponent_bits=8, mantissa_bits=7)


def head_lanes(head):
    lanes = lax.broadcasted_iota(jnp.int32, (1, 2 * HEAD_DIM), 1)
    return (lanes >= HEAD_DIM) if head else (lanes < HEAD_DIM)


def fill_mask(mask, seg_q, seg_k):
    for c in range(TB // CH):
        rows = lax.broadcasted_iota(jnp.int32, (CH, SPAN), 0)
        cols = lax.broadcasted_iota(jnp.int32, (CH, SPAN), 1)
        gap = rows + WINDOW - cols
        same = seg_q[c * CH : (c + 1) * CH, :] == seg_k[:, c * CH : c * CH + SPAN]
        keep = (gap >= 0) & (gap < WINDOW) & same
        mask[c] = jnp.where(keep, 0.0, MASKED)


def forward_kernel(
    q, k, v, k1, v1, k2, v2, gate, decay, seg_q, seg_k, att, gated, norm, keys, values, mask
):
    pair = pl.program_id(0)

    @pl.when(pair == 0)
    def _():
        fill_mask(mask, seg_q, seg_k)

    keys[0:TB, :] = k2[...]
    keys[TB : 2 * TB, :] = k1[...]
    keys[2 * TB :, :] = k[...]
    values[0:TB, :] = v2[...]
    values[TB : 2 * TB, :] = v1[...]
    values[2 * TB :, :] = v[...]
    lane = lax.broadcasted_iota(jnp.int32, (CH, 8), 1)
    for c in range(TB // CH):
        rows = slice(c * CH, (c + 1) * CH)
        span = slice(c * CH, c * CH + SPAN)
        mixed, norms = [], []
        for h in range(2):
            mine = head_lanes(h)
            q_h = jnp.where(mine, q[rows, :], jnp.zeros((), BF)) * jnp.asarray(HEAD_DIM**-0.5, BF)
            s = dot_t(q_h, keys[span, :]) - decay[pl.ds(2 * pair + h, 1), span] + mask[c]
            top = jnp.max(s, axis=1, keepdims=True)
            e = jnp.exp(s - top)
            total = jnp.sum(e, axis=1, keepdims=True)
            p = (e * (1.0 / total)).astype(BF)
            mixed.append(dot(p, values[span, :]))
            norms.append(top + jnp.log(total))
        out = jnp.where(head_lanes(0), mixed[0], mixed[1])
        att[rows, :] = out
        gated[rows, :] = (out * jax.nn.sigmoid(gate[rows, :])).astype(BF)
        norm[0, rows, :] = jnp.where(lane == 0, norms[0], norms[1])


def backward_kernel(
    q, k, v, k1, v1, k2, v2, grad_attended, decay, seg_q, seg_k, norm,
    dq, dk, dv, d1, d2, forget,
    keys, values, mask, dk_sum, dv_sum, col_sum, row_sum,
):
    pair = pl.program_id(0)
    lane = lax.broadcasted_iota(jnp.int32, (1, EXT), 1)

    @pl.when(pair == 0)
    def _():
        fill_mask(mask, seg_q, seg_k)
        col_sum[...] = jnp.zeros_like(col_sum)
        row_sum[...] = jnp.zeros_like(row_sum)

    keys[0:TB, :] = k2[...]
    keys[TB : 2 * TB, :] = k1[...]
    keys[2 * TB :, :] = k[...]
    values[0:TB, :] = v2[...]
    values[TB : 2 * TB, :] = v1[...]
    values[2 * TB :, :] = v[...]
    dk_sum[...] = jnp.zeros_like(dk_sum)
    dv_sum[...] = jnp.zeros_like(dv_sum)
    for c in range(TB // CH):
        rows = slice(c * CH, (c + 1) * CH)
        span = slice(c * CH, c * CH + SPAN)
        grad = grad_attended[rows, :]
        dq_parts = []
        for h in range(2):
            mine = head_lanes(h)
            marks = ((lane % HEADS_COL == 2 * pair + h) & (lane < 4 * HEADS_COL)).astype(F32)
            q_h = jnp.where(mine, q[rows, :], jnp.zeros((), BF)) * jnp.asarray(HEAD_DIM**-0.5, BF)
            g_h = jnp.where(mine, grad, jnp.zeros((), BF))
            s = dot_t(q_h, keys[span, :]) - decay[pl.ds(2 * pair + h, 1), span] + mask[c]
            p = jnp.exp(s - norm[0, rows, h : h + 1])
            dp = dot_t(g_h, values[span, :])
            total = jnp.sum(p * dp, axis=1, keepdims=True)
            ds = (p * (dp - total)).astype(BF)
            dq_parts.append(dot(ds, keys[span, :]))
            wide = t_dot(
                ds, jnp.concatenate([q_h, jnp.broadcast_to(marks, (CH, EXT)).astype(BF)], axis=1)
            )
            dk_sum[span, :] += wide[:, :128]
            col_sum[span, :] += wide[:, 128:]
            dv_sum[span, :] += t_dot(p.astype(BF), g_h)
            row_sum[rows, :] += jnp.sum(ds.astype(F32), axis=1, keepdims=True) * marks
        dq[rows, :] = (jnp.where(head_lanes(0), dq_parts[0], dq_parts[1]) * HEAD_DIM**-0.5).astype(BF)
    k_at = pl.ds(pl.multiple_of(pair * 128, 128), 128)
    v_at = pl.ds(pl.multiple_of(384 + pair * 128, 128), 128)
    d2[:, k_at] = dk_sum[0:TB, :].astype(BF)
    d2[:, v_at] = dv_sum[0:TB, :].astype(BF)
    d1[:, k_at] = dk_sum[TB : 2 * TB, :].astype(BF)
    d1[:, v_at] = dv_sum[TB : 2 * TB, :].astype(BF)
    dk[...] = dk_sum[2 * TB :, :]
    dv[...] = dv_sum[2 * TB :, :]

    @pl.when(pair == pl.num_programs(0) - 1)
    def _():
        forget[...] = row_sum[...] - col_sum[2 * TB :, :]

        def parts(value):
            high = value.astype(BF).astype(F32)
            return jnp.where((lane // HEADS_COL) % 2 == 0, high, value - high)

        far, near = col_sum[0:TB, :], col_sum[TB : 2 * TB, :]
        all_far = jnp.sum(far, axis=0, keepdims=True)
        d2[:, 768:] = jnp.where(lane < 2 * HEADS_COL, parts(far), 0.0).astype(BF)
        d1[:, 768:] = jnp.where(lane < 2 * HEADS_COL, parts(near), parts(all_far)).astype(BF)


def pair_block(rows, offset=0):
    return pl.BlockSpec((rows, 128), lambda p, offset=offset: (0, p + offset))


def whole(*shape):
    return pl.BlockSpec(shape, lambda p: (0,) * len(shape))


def per_pair(*shape):
    return pl.BlockSpec((1,) + shape, lambda p: (p,) + (0,) * len(shape))


def attention_inputs():
    return [
        pair_block(TB, 0), pair_block(TB, 3), pair_block(TB, 6),
        pair_block(TB, 0), pair_block(TB, 3), pair_block(TB, 0), pair_block(TB, 3),
        pair_block(TB), whole(8, KW), whole(TB, 1), whole(1, KW),
    ]


PARAMS = pltpu.CompilerParams(vmem_limit_bytes=48 * 1024 * 1024, dimension_semantics=("arbitrary",))


def attend(qkv, halo1, halo2, gate, decay, seg_q, seg_k):
    pairs = 3
    return pl.pallas_call(
        forward_kernel,
        grid=(pairs,),
        in_specs=attention_inputs(),
        out_specs=[pair_block(TB), pair_block(TB), per_pair(TB, 8)],
        out_shape=[
            jax.ShapeDtypeStruct((TB, pairs * 128), F32),
            jax.ShapeDtypeStruct((TB, pairs * 128), BF),
            jax.ShapeDtypeStruct((pairs, TB, 8), F32),
        ],
        scratch_shapes=[
            pltpu.VMEM((KW, 128), BF), pltpu.VMEM((KW, 128), BF),
            pltpu.VMEM((TB // CH, CH, SPAN), F32),
        ],
        compiler_params=PARAMS,
        cost_estimate=pl.CostEstimate(flops=2_400_000_000, bytes_accessed=8_000_000, transcendentals=4_000_000),
        name="attend",
    )(qkv, qkv, qkv, halo1, halo1, halo2, halo2, gate, decay, seg_q, seg_k)


def attend_back(qkv, halo1, halo2, grad_attended, decay, seg_q, seg_k, norm):
    pairs = 3
    return pl.pallas_call(
        backward_kernel,
        grid=(pairs,),
        in_specs=attention_inputs() + [per_pair(TB, 8)],
        out_specs=[
            pair_block(TB), pair_block(TB), pair_block(TB), whole(TB, 896), whole(TB, 896),
            whole(TB, EXT),
        ],
        out_shape=[
            jax.ShapeDtypeStruct((TB, pairs * 128), BF),
            jax.ShapeDtypeStruct((TB, pairs * 128), F32),
            jax.ShapeDtypeStruct((TB, pairs * 128), F32),
            jax.ShapeDtypeStruct((TB, 896), BF),
            jax.ShapeDtypeStruct((TB, 896), BF),
            jax.ShapeDtypeStruct((TB, EXT), F32),
        ],
        scratch_shapes=[
            pltpu.VMEM((KW, 128), BF), pltpu.VMEM((KW, 128), BF),
            pltpu.VMEM((TB // CH, CH, SPAN), F32),
            pltpu.VMEM((KW, 128), F32), pltpu.VMEM((KW, 128), F32),
            pltpu.VMEM((KW, EXT), F32), pltpu.VMEM((TB, EXT), F32),
        ],
        compiler_params=PARAMS,
        cost_estimate=pl.CostEstimate(flops=6_000_000_000, bytes_accessed=14_000_000, transcendentals=4_000_000),
        name="attend_back",
    )(qkv, qkv, qkv, halo1, halo1, halo2, halo2, grad_attended, decay, seg_q, seg_k, norm)


def one_hot(bases, j, features):
    at = lax.broadcasted_iota(jnp.int32, (WIDE, features.shape[1]), 0)
    piece = at + jnp.where(at < SHARD, bases[j], bases[PIECES + j] - SHARD)
    return (piece == features).astype(F32).astype(BF)


def arrange_kernel(*refs):
    bases, features = refs[0], refs[1]
    pieces = refs[2 : 2 + PIECES]
    source, normed, cot, gains, inverse, wide = refs[2 + PIECES :]

    @pl.when(pl.program_id(0) == 0)
    def _():
        total = jnp.zeros((TB, 1), F32)
        for j in range(PIECES):
            wide[:, j * WIDE : (j + 1) * WIDE] = pieces[j][...]
            rows = pieces[j][:TB, :].astype(F32)
            total = total + jnp.sum(rows * rows, axis=1, keepdims=True)
        inverse[...] = lax.rsqrt(total / D + EPS)

    hot = jnp.concatenate([one_hot(bases, j, features[...]) for j in range(PIECES)], axis=0)
    rows = dot(wide[TB:, :], hot)
    cot[...] = rows[:QUARTER].astype(BF)
    gains[...] = rows[QUARTER : QUARTER + 8]
    gain = rows[QUARTER : QUARTER + 1]
    for c in range(TB // CH):
        at = slice(c * CH, (c + 1) * CH)
        rows = dot(wide[at, :], hot)
        source[at, :] = rows.astype(BF)
        normed[at, :] = (rows * inverse[at, :] * gain).astype(BF)


def arrange(bases, features, pieces):
    def tile(rows):
        return pl.BlockSpec((rows, TILE), lambda n: (0, n))

    return pl.pallas_call(
        arrange_kernel,
        grid=(D // TILE,),
        in_specs=[pl.BlockSpec(memory_space=pltpu.SMEM), tile(1)] + [whole(ROWS_IN, WIDE)] * PIECES,
        out_specs=[tile(TB), tile(TB), tile(QUARTER), tile(8), whole(TB, 1)],
        out_shape=[
            jax.ShapeDtypeStruct((TB, D), BF),
            jax.ShapeDtypeStruct((TB, D), BF),
            jax.ShapeDtypeStruct((QUARTER, D), BF),
            jax.ShapeDtypeStruct((8, D), F32),
            jax.ShapeDtypeStruct((TB, 1), F32),
        ],
        scratch_shapes=[pltpu.VMEM((ROWS_IN, D), BF)],
        compiler_params=PARAMS,
        cost_estimate=pl.CostEstimate(flops=4_000_000_000, bytes_accessed=6_000_000, transcendentals=512),
        name="arrange",
    )(bases, features, *pieces)


def release_kernel(
    bases, features, partial, source, inverse, gain, grad_residual, output, piece, rows
):
    @pl.when(pl.program_id(0) == 0)
    def _():
        for c in range(GROUP_COLS):
            at = slice(c * QUARTER, (c + 1) * QUARTER)
            scaled = gain[...] * partial[at, :]
            values = source[at, :].astype(F32)
            scale = inverse[at, :]
            total = jnp.sum(scaled * values, axis=1, keepdims=True)
            part = scale * scaled - values * (scale * scale * scale * total / D)
            part = part + jnp.where(c == bases[2 * PIECES], grad_residual[...], 0.0)
            rows[at, :] = part.astype(BF)
        rows[TB:, :] = output[...]

    piece[0] = dot_t(rows[...], one_hot(bases, pl.program_id(0), features[...])).astype(BF)


def release(bases, features, partial, source, inverse, gain, grad_residual, output):
    return pl.pallas_call(
        release_kernel,
        grid=(PIECES,),
        in_specs=[
            pl.BlockSpec(memory_space=pltpu.SMEM), whole(1, D), whole(TB, D), whole(TB, D),
            whole(TB, 1), whole(1, D), whole(QUARTER, D), whole(QUARTER, D),
        ],
        out_specs=per_pair(ROWS_OUT, WIDE),
        out_shape=jax.ShapeDtypeStruct((PIECES, ROWS_OUT, WIDE), BF),
        scratch_shapes=[pltpu.VMEM((ROWS_OUT, D), BF)],
        compiler_params=PARAMS,
        cost_estimate=pl.CostEstimate(flops=4_000_000_000, bytes_accessed=8_000_000, transcendentals=512),
        name="release",
    )(bases, features, partial, source, inverse, gain, grad_residual, output)


def gather_x(both):
    return lax.all_gather(both, "x", axis=0, tiled=True)


def scatter_x(mine):
    return lax.psum_scatter(mine, "x", scatter_dimension=0, tiled=True)


def by_rows(matrix):
    return with_layout_constraint(matrix, Layout(major_to_minor=(0, 1)))


def with_partner(shard):
    return jnp.concatenate([shard, z_partner(shard)], axis=0)


def tie(*values):
    return lax.optimization_barrier(values)


def after(value, *others):
    return tie(value, *others)[0]


def leaving_rows(left, right):
    return t_dot(left[:, D // 2 :], right).astype(BF)


def summed_rows(left, right, arrived):
    return (t_dot(left[:, : D // 2], right) + arrived.astype(F32)).astype(BF)


def near_sum(part):
    rows = part.shape[0] // 2
    return part[:rows].astype(F32) + z_partner(part[rows:]).astype(F32)


def twin_sum(part):
    return rounded(part) + z_twin(rounded(part).astype(BF)).astype(F32)


def both_halves(part, other, core):
    part = rounded(part).astype(BF)
    return jnp.where(
        core == 0, jnp.concatenate([part, other], axis=0), jnp.concatenate([other, part], axis=0)
    ).astype(F32)


def reorder(pieces, key):
    return [lax.dynamic_index_in_dim(pieces, i ^ key, 0, keepdims=False) for i in range(pieces.shape[0])]


def body(
    block_input,
    attn_gain,
    attn_weight,
    forget_weight,
    forget_bias,
    out_weight,
    ffn_gain,
    gate_up_weight,
    down_weight,
    segments,
    cotangent,
):
    core = lax.axis_index("core")
    zh = lax.axis_index("zh")
    x = lax.axis_index("x")
    y = lax.axis_index("y")
    heads = forget_weight.shape[1]
    width = heads * HEAD_DIM
    ffn = down_weight.shape[0]
    shard = block_input.shape[1]
    half = shard // 2

    side = x % 2
    spot = 2 * zh + x // 2

    def half_rows(index):
        return [lax.dynamic_slice_in_dim(rows, index * TB, TB, 0) for rows in (block_input, cotangent)]

    gain_rows = jnp.pad(jnp.stack([attn_gain, ffn_gain]), ((0, 14), (0, 0)))
    far_rows = x_flip(jnp.concatenate(half_rows(1 - side) + [gain_rows], axis=0), 1)
    extra = jnp.pad(jnp.concatenate([forget_weight] * 3, axis=1), ((0, 0), (0, EXT - 3 * heads)))
    proj_cols = 4 * width + EXT

    def mine(rows):
        return lax.dynamic_slice_in_dim(rows, core * half, half, 0)

    first_both = with_partner(
        jnp.concatenate(
            [mine(attn_weight.reshape(shard, 4 * width)), mine(extra), mine(out_weight.T)], axis=1
        )
    )
    first_both = after(first_both, far_rows)
    wide_rows = jnp.concatenate(
        [jnp.concatenate(half_rows(side) + [gain_rows], axis=0), far_rows], axis=1
    )

    def leaving_tokens(step):
        return jnp.concatenate(
            [
                wide_rows[:TB],
                lax.dynamic_slice_in_dim(wide_rows, TB + (spot ^ step) * QUARTER, QUARTER, 0),
                wide_rows[2 * TB :],
            ]
        )

    arrived = [lax.ppermute(leaving_tokens(j), ALL, to_groups(j)) for j in range(PIECES)]

    first_half = gather_x(first_both)
    ffn_both = with_partner(
        jnp.concatenate(
            [mine(gate_up_weight.reshape(shard, 2 * ffn)), mine(down_weight.T)], axis=1
        )
    )
    other_segments = core_flip(segments)

    col_at = jnp.arange(D, dtype=jnp.int32)
    block = col_at // half
    features = (
        ((zh ^ (block % 2)) * 4 + (block // 2) % 4) * shard
        + (core ^ (block // 8)) * half + col_at % half
    )[None, :]
    spots = jnp.arange(PIECES, dtype=jnp.int32) ^ y
    rows_x = (spots // 2) * 4 + 2 * (spots % 2)
    bases = jnp.concatenate(
        [(rows_x + side) * shard, (rows_x + 1 - side) * shard, y[None].astype(jnp.int32)]
    )
    source_low, normed, cot_mine, gains, inverse_first = arrange(bases, features, arrived)
    gain_first, gain_second = gains[0:1], gains[1:2]
    first_half, ffn_both, other_segments, normed = tie(
        first_half, ffn_both, other_segments, normed
    )

    first_other = core_flip(first_half)
    w_proj = jnp.concatenate([first_half, first_other], axis=0)
    out_half = first_half[:, proj_cols:]
    out_others = [y_flip(out_half, d) for d in range(1, 4)]
    projected = dot(normed[:, : D // 2], first_half) + dot(normed[:, D // 2 :], first_other)
    qkv = projected[:, : 3 * width].astype(BF)
    lanes = lax.broadcasted_iota(jnp.int32, (1, EXT), 1)
    earlier = (
        lax.broadcasted_iota(jnp.int32, (TB, TB), 0) >= lax.broadcasted_iota(jnp.int32, (TB, TB), 1)
    ).astype(F32)
    bias_lanes = jnp.pad(jnp.concatenate([forget_bias] * 3), (0, EXT - 3 * heads))[None, :]
    gate_logit = projected[:, 3 * width : 4 * width]
    forget_lanes = projected[:, 4 * width : proj_cols] + bias_lanes
    cumulative = jnp.dot(earlier, jax.nn.log_sigmoid(forget_lanes), precision=HIGHEST)
    rest = cumulative - rounded(cumulative)
    parts = jnp.where(
        lanes < heads, cumulative, jnp.where(lanes < 2 * heads, rest, rest - rounded(rest))
    ).astype(BF)

    sequence_block = 2 * core + x % 2
    key_values = jnp.concatenate([qkv[:, width:], parts], axis=1)
    halo1 = block_shift(key_values, 1)
    halo2 = block_shift(key_values, 2)
    cot_leaving = after(cot_mine, key_values)
    cot_others = [y_flip(cot_leaving, d) for d in range(1, 4)]
    own = jnp.where(x // 2 == core, segments, other_segments)
    own = lax.dynamic_index_in_dim(own, zh, 0, keepdims=False)
    padded = jnp.concatenate([jnp.full((2 * TB,), -1, jnp.int32), own])
    seg_k = lax.dynamic_slice_in_dim(padded, sequence_block * TB, KW)
    seg_q = lax.dynamic_slice_in_dim(own, sequence_block * TB, TB)[:, None]
    seg_k = seg_k[None, :]
    out_half = jnp.concatenate([out_half] + out_others, axis=1)
    halo1, halo2, qkv, gate_logit, seg_q, seg_k, out_half = tie(
        halo1, halo2, qkv, gate_logit, seg_q, seg_k, out_half
    )
    out_other = core_flip(out_half)
    ffn_half = gather_x(after(ffn_both, halo1))
    column = lax.broadcasted_iota(jnp.int32, (EXT, 8), 1)
    lane_at = lax.broadcasted_iota(jnp.int32, (EXT, 8), 0)
    gather_parts = ((lane_at % heads == column) & (lane_at < 3 * heads)).astype(BF)
    decay = lax.dot_general(
        gather_parts,
        jnp.concatenate([halo2[:, 2 * width :], halo1[:, 2 * width :], parts], axis=0),
        (((0,), (1,)), ((), ())),
        preferred_element_type=F32,
    )
    last1 = decay[:, 2 * TB - 1 : 2 * TB]
    last2 = decay[:, TB - 1 : TB] + last1
    key_at = lax.broadcasted_iota(jnp.int32, (1, KW), 1)
    decay = decay - jnp.where(key_at < TB, last2, jnp.where(key_at < 2 * TB, last1, 0.0))
    attended, gated, norm = attend(qkv, halo1, halo2, gate_logit, decay, seg_q, seg_k)
    gated, out_other, *cot_others = tie(gated, out_other, *cot_others)
    gated_others = [y_flip(gated, d) for d in range(1, 4)]
    w_out = tie(jnp.concatenate([out_half, out_other], axis=0))[0]
    ffn_half = after(ffn_half, *gated_others)
    w_ffn = jnp.concatenate([ffn_half, core_flip(ffn_half)], axis=0)
    w_gate_up, w_down = w_ffn[:, : 2 * ffn], w_ffn[:, 2 * ffn :]
    cot = jnp.concatenate(reorder(jnp.stack([cot_mine] + cot_others), y), axis=0)

    gated_all = jnp.concatenate([gated] + gated_others, axis=1)
    residual = source_low.astype(F32) + dot_t(gated_all, w_out)
    inverse_second = lax.rsqrt(jnp.mean(residual * residual, axis=1, keepdims=True) + EPS)
    normed_second = (residual * inverse_second * gain_second).astype(BF)
    gate_up = dot(normed_second, w_gate_up)
    gate_rows, up_rows = gate_up[:, :ffn], gate_up[:, ffn:]
    ffn_open = jax.nn.sigmoid(gate_rows)
    hidden = (gate_rows * ffn_open * up_rows).astype(BF)
    grad_hidden = dot(cot, w_down)
    grad_gate_up = jnp.concatenate(
        [
            (grad_hidden * up_rows * ffn_open * (1.0 + gate_rows * (1.0 - ffn_open))).astype(BF),
            (grad_hidden * gate_rows * ffn_open).astype(BF),
        ],
        axis=1,
    )

    def rows_of(matrix, index):
        return lax.dynamic_slice_in_dim(matrix, index * QUARTER, QUARTER, 0)

    def others_rows(partial):
        return [y_flip(rows_of(partial, y ^ d).astype(BF), d) for d in range(1, 4)]

    def summed(first, others):
        return first + sum(other.astype(F32) for other in others)

    partial_second = dot_t(grad_gate_up, w_gate_up)
    second_others = others_rows(partial_second)
    second_mine = rows_of(partial_second, y)

    gate_up_arrived = core_flip(leaving_rows(normed_second, grad_gate_up))
    down_arrived = core_flip(leaving_rows(cot, hidden))
    gate_up_mine = summed_rows(normed_second, grad_gate_up, gate_up_arrived)
    down_mine = summed_rows(cot, hidden, down_arrived)
    ffn_mine, *second_others = tie(
        jnp.concatenate([gate_up_mine, down_mine], axis=1), *second_others
    )
    ffn_scattered = scatter_x(ffn_mine)
    output_partial = dot_t(hidden, w_down)
    output_mine = rows_of(output_partial, y)
    output_leaving = [rows_of(output_partial, y ^ d).astype(BF) for d in range(1, 4)]
    second_others[0], output_mine, *output_leaving = tie(
        second_others[0], output_mine, *output_leaving
    )
    grad_normed_second = summed(second_mine, second_others)
    residual_mine = rows_of(residual, y)
    inverse_mine = rows_of(inverse_second, y)
    scaled = gain_second * grad_normed_second
    second_dot = jnp.sum(scaled * residual_mine, axis=1, keepdims=True)
    grad_residual = (
        cot_mine.astype(F32)
        + inverse_mine * scaled
        - residual_mine * (inverse_mine**3 * second_dot / D)
    )
    grad_branch = grad_residual.astype(BF)
    grad_gated_all = dot(grad_branch, w_out).astype(BF)
    gated_pieces = jnp.stack(
        [grad_gated_all[:, :width]]
        + [y_flip(grad_gated_all[:, d * width : (d + 1) * width], d) for d in range(1, 4)]
    )
    grad_gated = jnp.concatenate(reorder(gated_pieces, y), axis=0).astype(F32)
    grad_gated, grad_branch = tie(grad_gated, grad_branch)
    branch_others = [y_flip(grad_branch, d) for d in range(1, 4)]

    gate_open = jax.nn.sigmoid(gate_logit)
    grad_attended = (grad_gated * gate_open).astype(BF)
    dgate = (grad_gated * attended * gate_open * (1.0 - gate_open)).astype(BF)
    dq, dk, dv, d1, d2, forget_part = attend_back(
        qkv, halo1, halo2, grad_attended, decay, seg_q, seg_k, norm
    )
    d1, d2, dgate, ffn_scattered, *others = tie(
        d1, d2, dgate, ffn_scattered, *output_leaving, *branch_others
    )
    output_leaving, branch_others = others[:3], others[3:]
    back1 = block_shift(d1, -1)
    back2 = block_shift(d2, -2)
    output_others = [y_flip(output_leaving[d - 1], d) for d in range(1, 4)]

    grad_branch, dgate, dq, *branch_others = tie(grad_branch, dgate, dq, *branch_others, back2)[:-1]
    partial_early = dot_t(dq, w_proj[:, :width]) + dot_t(dgate, w_proj[:, 3 * width : 4 * width])
    branch_rows = jnp.concatenate([grad_branch] + branch_others, axis=0)
    gated_rows = jnp.concatenate([rows_of(gated, y ^ d) for d in range(4)], axis=0)
    sooner = jnp.concatenate([dgate, dq], axis=1)
    sooner_leaving = jnp.concatenate(
        [leaving_rows(branch_rows, gated_rows), leaving_rows(normed, sooner)], axis=1
    )
    ffn_near = near_sum(after(ffn_scattered, back2))
    back1, back2, ffn_near, sooner_leaving, *output_others = tie(
        back1, back2, ffn_near, sooner_leaving, *output_others
    )
    ffn_part = twin_sum(ffn_near)
    back1, back2 = back1.astype(F32), back2.astype(F32)
    key_sums = back1[:, : 2 * width] + back2[:, : 2 * width]
    output_mine = (residual_mine + summed(output_mine, output_others)).astype(BF)

    from_lane = lax.broadcasted_iota(jnp.int32, (EXT, 1), 0)
    same_head = (from_lane % heads == lanes % heads) & (lanes < 2 * heads)
    join = (same_head & (from_lane < 2 * heads)).astype(F32)
    join_far = (same_head & (from_lane >= 2 * heads) & (from_lane < 4 * heads)).astype(F32)
    sums1, sums2 = back1[:, 2 * width :], back2[:, 2 * width :]
    other_sums = jnp.dot(sums1 + sums2, join, precision=HIGHEST)
    later = jnp.sum(other_sums, axis=0, keepdims=True) + jnp.dot(
        sums1[:1], join_far, precision=HIGHEST
    )
    suffix = lax.dot_general(
        earlier, forget_part - other_sums, (((0,), (0,)), ((), ())), precision=HIGHEST
    ) + later
    grad_forget = suffix * jax.nn.sigmoid(-forget_lanes)
    grad_extra = jnp.where(
        lanes < heads, grad_forget, jnp.where(lanes < 2 * heads, grad_forget - rounded(grad_forget), 0.0)
    ).astype(BF)
    dk_all = (dk + key_sums[:, :width]).astype(BF)
    dv_all = (dv + key_sums[:, width:]).astype(BF)

    bias_sum = jnp.broadcast_to(jnp.sum(grad_forget, axis=0, keepdims=True), (8, EXT))
    for other in (core_flip, lambda v: x_flip(v, 1), lambda v: x_flip(v, 2), z_partner, z_twin):
        bias_sum = bias_sum + other(bias_sum)
    late = jnp.concatenate([dk_all, dv_all, grad_extra], axis=1)
    leaving_late = leaving_rows(normed, late)
    attn_arrived = core_flip(by_rows(jnp.concatenate([sooner_leaving, leaving_late], axis=1)))
    early_cols = 3 * width
    attn_mine = jnp.concatenate(
        [
            summed_rows(branch_rows, gated_rows, attn_arrived[:, :width]),
            summed_rows(normed, sooner, attn_arrived[:, width:early_cols]),
            summed_rows(normed, late, attn_arrived[:, early_cols:]),
        ],
        axis=1,
    )
    attn_scattered = scatter_x(by_rows(attn_mine))
    partial_first = (
        partial_early
        + dot_t(late[:, : 2 * width], w_proj[:, width : 3 * width])
        + dot_t(grad_extra, w_proj[:, 4 * width : proj_cols])
    )

    leaving = release(
        bases, features, partial_first, source_low, inverse_first, gain_first, grad_residual, output_mine
    )
    ffn_other = core_flip(rounded(ffn_part).astype(BF))
    leaving, ffn_part, ffn_other = tie(leaving, ffn_part, ffn_other)
    returned = [lax.ppermute(leaving[j], ALL, from_groups(j)) for j in range(PIECES)]
    attn_part = twin_sum(near_sum(attn_scattered))
    bias_sum, *returned = tie(bias_sum, *returned)
    input_rows = sum(piece[:TB].astype(F32) for piece in returned)
    output_rows = jnp.concatenate(reorder(jnp.stack([piece[TB:] for piece in returned]), spot), axis=0)
    far_rows = x_flip(
        jnp.concatenate([input_rows[:, shard:].astype(BF), output_rows[:, shard:]], axis=0), 1
    )
    near, far = input_rows[:, :shard], far_rows[:TB].astype(F32)
    input_grad = jnp.concatenate(
        [jnp.where(side == 0, near, far), jnp.where(side == 0, far, near)], axis=0
    )
    near, far = output_rows[:, :shard], far_rows[TB:]
    block_output = jnp.concatenate(
        [jnp.where(side == 0, near, far), jnp.where(side == 0, far, near)], axis=0
    )

    ffn_full = both_halves(ffn_part, ffn_other, core)
    attn_all = both_halves(attn_part, core_flip(rounded(attn_part).astype(BF)), core)
    extras = attn_all[:, 5 * width :]
    forget_grad = extras[:, :heads] + extras[:, heads : 2 * heads]
    attn_full = jnp.concatenate(
        [attn_all[:, 2 * width : 5 * width], attn_all[:, width : 2 * width]], axis=1
    )

    def row_dot(weight, grad):
        return jnp.sum(mine(weight).astype(F32) * grad, axis=1)

    gain_parts = jnp.stack(
        [
            (
                row_dot(attn_weight[:, :3].reshape(shard, 3 * width), attn_part[:, 2 * width : 5 * width])
                + row_dot(attn_weight[:, 3], attn_part[:, width : 2 * width])
                + row_dot(
                    jnp.concatenate([forget_weight] * 2, axis=1),
                    attn_part[:, 5 * width : 5 * width + 2 * heads],
                )
            )
            / mine(attn_gain).astype(F32),
            row_dot(gate_up_weight.reshape(shard, 2 * ffn), ffn_part[:, : 2 * ffn])
            / mine(ffn_gain).astype(F32),
        ]
    )
    gain_others = [y_flip(gain_parts, d) for d in range(1, 4)]
    gain_half = (gain_parts + gain_others[0]) + (gain_others[1] + gain_others[2])
    gain_other = core_flip(gain_half)
    gain_sum = jnp.where(
        core == 0,
        jnp.concatenate([gain_half, gain_other], axis=1),
        jnp.concatenate([gain_other, gain_half], axis=1),
    )
    return (
        block_output,
        input_grad,
        gain_sum[0],
        attn_full.reshape(attn_weight.shape),
        forget_grad,
        bias_sum[0, :heads],
        attn_all[:, :width].T,
        gain_sum[1],
        ffn_full[:, : 2 * ffn].reshape(gate_up_weight.shape),
        ffn_full[:, 2 * ffn :].T,
    )


def solution(mesh):
    inner = Mesh(mesh.devices.reshape(DIMS), ALL)
    dp, row = ("zl", "core"), ("zh", "x")
    tokens = P(("zl", "core", "y"), row)
    in_specs = (
        tokens, P(row), P(row, None, "y"), P(row, "y"), P("y"), P("y", row), P(row),
        P(row, None, "y"), P("y", row), P(dp, None), tokens,
    )
    out_specs = (
        tokens, tokens, P(row), P(row, None, "y"), P(row, "y"), P("y"), P("y", row), P(row),
        P(row, None, "y"), P("y", row),
    )
    return jax.shard_map(body, mesh=inner, in_specs=in_specs, out_specs=out_specs, check_vma=False)
```

```python
import jax
import jax.numpy as jnp
from jax import lax
from jax.experimental import pallas as pl
from jax.experimental.layout import Layout, with_layout_constraint
from jax.experimental.pallas import tpu as pltpu
from jax.sharding import Mesh, PartitionSpec as P

D = 1536
HEAD_DIM = 64
WINDOW = 1024
EPS = 1e-06
MASKED = -1e30
ALL = ("zl", "core", "zh", "x", "y")
DIMS = (2, 2, 2, 4, 4)
BF = jnp.bfloat16
F32 = jnp.float32
HIGHEST = lax.Precision.HIGHEST

TB = 512
KW = 3 * TB
CH = 128
SPAN = WINDOW + CH
GROUP_COLS = 4
EXT = 128
HEADS_COL = 6
PIECES = 4
SHARD = D // 8
WIDE = 2 * SHARD
QUARTER = TB // GROUP_COLS
ROWS_IN = TB + QUARTER + 16
ROWS_OUT = TB + QUARTER
TILE = 256


def place(zl, core, zh, x, y):
    return (((zl * 2 + core) * 2 + zh) * 4 + x) * 4 + y


def places():
    for zl in range(2):
        for core in range(2):
            for zh in range(2):
                for x in range(4):
                    for y in range(4):
                        yield zl, core, zh, x, y


def to_groups(step):
    return [
        (
            place(zl, core, zh, x, y),
            place(zl, y % 2, y // 2, 2 * core + x % 2, (2 * zh + x // 2) ^ step),
        )
        for zl, core, zh, x, y in places()
    ]


def from_groups(step):
    return [(target, source) for source, target in to_groups(step)]


def flip(value, axis, size, bits):
    return lax.ppermute(value, axis, [(i, i ^ bits) for i in range(size)])


def core_flip(value):
    return flip(value, "core", 2, 1)


def z_partner(value):
    return flip(value, ("zl", "zh"), 4, 3)


def zh_flip(value):
    return flip(value, "zh", 2, 1)


def z_twin(value):
    return flip(value, "zl", 2, 1)


def x_flip(value, bits):
    return flip(value, "x", 4, bits)


def y_flip(value, bits):
    return flip(value, "y", 4, bits)


def block_shift(value, distance):
    pairs = []
    for core in range(2):
        for x in range(4):
            block = 2 * core + x % 2
            other = block + distance
            if 0 <= other < 4:
                pairs.append((core * 4 + x, (other // 2) * 4 + (x // 2) * 2 + other % 2))
    return lax.ppermute(value, ("core", "x"), pairs)


def dot(a, b):
    return lax.dot_general(a, b, (((1,), (0,)), ((), ())), preferred_element_type=F32)


def dot_t(a, b):
    return lax.dot_general(a, b, (((1,), (1,)), ((), ())), preferred_element_type=F32)


def t_dot(a, b):
    return lax.dot_general(a, b, (((0,), (0,)), ((), ())), preferred_element_type=F32)


def rounded(value):
    return lax.reduce_precision(value, exponent_bits=8, mantissa_bits=7)


def head_lanes(head):
    lanes = lax.broadcasted_iota(jnp.int32, (1, 2 * HEAD_DIM), 1)
    return (lanes >= HEAD_DIM) if head else (lanes < HEAD_DIM)


def fill_mask(mask, seg_q, seg_k):
    for c in range(TB // CH):
        rows = lax.broadcasted_iota(jnp.int32, (CH, SPAN), 0)
        cols = lax.broadcasted_iota(jnp.int32, (CH, SPAN), 1)
        gap = rows + WINDOW - cols
        same = seg_q[c * CH : (c + 1) * CH, :] == seg_k[:, c * CH : c * CH + SPAN]
        keep = (gap >= 0) & (gap < WINDOW) & same
        mask[c] = jnp.where(keep, 0.0, MASKED)


def forward_kernel(
    q, k, v, k1, v1, k2, v2, gate, decay, seg_q, seg_k, att, gated, norm, keys, values, mask
):
    pair = pl.program_id(0)

    @pl.when(pair == 0)
    def _():
        fill_mask(mask, seg_q, seg_k)

    keys[0:TB, :] = k2[...]
    keys[TB : 2 * TB, :] = k1[...]
    keys[2 * TB :, :] = k[...]
    values[0:TB, :] = v2[...]
    values[TB : 2 * TB, :] = v1[...]
    values[2 * TB :, :] = v[...]
    lane = lax.broadcasted_iota(jnp.int32, (CH, 8), 1)
    for c in range(TB // CH):
        rows = slice(c * CH, (c + 1) * CH)
        span = slice(c * CH, c * CH + SPAN)
        mixed, norms = [], []
        for h in range(2):
            mine = head_lanes(h)
            q_h = jnp.where(mine, q[rows, :], jnp.zeros((), BF)) * jnp.asarray(HEAD_DIM**-0.5, BF)
            s = dot_t(q_h, keys[span, :]) - decay[pl.ds(2 * pair + h, 1), span] + mask[c]
            top = jnp.max(s, axis=1, keepdims=True)
            e = jnp.exp(s - top)
            total = jnp.sum(e, axis=1, keepdims=True)
            p = (e * (1.0 / total)).astype(BF)
            mixed.append(dot(p, values[span, :]))
            norms.append(top + jnp.log(total))
        out = jnp.where(head_lanes(0), mixed[0], mixed[1])
        att[rows, :] = out
        gated[rows, :] = (out * jax.nn.sigmoid(gate[rows, :])).astype(BF)
        norm[0, rows, :] = jnp.where(lane == 0, norms[0], norms[1])


def backward_kernel(
    q, k, v, k1, v1, k2, v2, grad_attended, decay, seg_q, seg_k, norm,
    dq, dk, dv, d1, d2, forget,
    keys, values, mask, dk_sum, dv_sum, col_sum, row_sum,
):
    pair = pl.program_id(0)
    lane = lax.broadcasted_iota(jnp.int32, (1, EXT), 1)

    @pl.when(pair == 0)
    def _():
        fill_mask(mask, seg_q, seg_k)
        col_sum[...] = jnp.zeros_like(col_sum)
        row_sum[...] = jnp.zeros_like(row_sum)

    keys[0:TB, :] = k2[...]
    keys[TB : 2 * TB, :] = k1[...]
    keys[2 * TB :, :] = k[...]
    values[0:TB, :] = v2[...]
    values[TB : 2 * TB, :] = v1[...]
    values[2 * TB :, :] = v[...]
    dk_sum[...] = jnp.zeros_like(dk_sum)
    dv_sum[...] = jnp.zeros_like(dv_sum)
    for c in range(TB // CH):
        rows = slice(c * CH, (c + 1) * CH)
        span = slice(c * CH, c * CH + SPAN)
        grad = grad_attended[rows, :]
        dq_parts = []
        for h in range(2):
            mine = head_lanes(h)
            marks = ((lane % HEADS_COL == 2 * pair + h) & (lane < 4 * HEADS_COL)).astype(F32)
            q_h = jnp.where(mine, q[rows, :], jnp.zeros((), BF)) * jnp.asarray(HEAD_DIM**-0.5, BF)
            g_h = jnp.where(mine, grad, jnp.zeros((), BF))
            s = dot_t(q_h, keys[span, :]) - decay[pl.ds(2 * pair + h, 1), span] + mask[c]
            p = jnp.exp(s - norm[0, rows, h : h + 1])
            dp = dot_t(g_h, values[span, :])
            total = jnp.sum(p * dp, axis=1, keepdims=True)
            ds = (p * (dp - total)).astype(BF)
            dq_parts.append(dot(ds, keys[span, :]))
            wide = t_dot(
                ds, jnp.concatenate([q_h, jnp.broadcast_to(marks, (CH, EXT)).astype(BF)], axis=1)
            )
            dk_sum[span, :] += wide[:, :128]
            col_sum[span, :] += wide[:, 128:]
            dv_sum[span, :] += t_dot(p.astype(BF), g_h)
            row_sum[rows, :] += jnp.sum(ds.astype(F32), axis=1, keepdims=True) * marks
        dq[rows, :] = (jnp.where(head_lanes(0), dq_parts[0], dq_parts[1]) * HEAD_DIM**-0.5).astype(BF)
    k_at = pl.ds(pl.multiple_of(pair * 128, 128), 128)
    v_at = pl.ds(pl.multiple_of(384 + pair * 128, 128), 128)
    d2[:, k_at] = dk_sum[0:TB, :].astype(BF)
    d2[:, v_at] = dv_sum[0:TB, :].astype(BF)
    d1[:, k_at] = dk_sum[TB : 2 * TB, :].astype(BF)
    d1[:, v_at] = dv_sum[TB : 2 * TB, :].astype(BF)
    dk[...] = dk_sum[2 * TB :, :]
    dv[...] = dv_sum[2 * TB :, :]

    @pl.when(pair == pl.num_programs(0) - 1)
    def _():
        forget[...] = row_sum[...] - col_sum[2 * TB :, :]

        def parts(value):
            high = value.astype(BF).astype(F32)
            return jnp.where((lane // HEADS_COL) % 2 == 0, high, value - high)

        far, near = col_sum[0:TB, :], col_sum[TB : 2 * TB, :]
        all_far = jnp.sum(far, axis=0, keepdims=True)
        d2[:, 768:] = jnp.where(lane < 2 * HEADS_COL, parts(far), 0.0).astype(BF)
        d1[:, 768:] = jnp.where(lane < 2 * HEADS_COL, parts(near), parts(all_far)).astype(BF)


def pair_block(rows, offset=0):
    return pl.BlockSpec((rows, 128), lambda p, offset=offset: (0, p + offset))


def whole(*shape):
    return pl.BlockSpec(shape, lambda p: (0,) * len(shape))


def per_pair(*shape):
    return pl.BlockSpec((1,) + shape, lambda p: (p,) + (0,) * len(shape))


def attention_inputs():
    return [
        pair_block(TB, 0), pair_block(TB, 3), pair_block(TB, 6),
        pair_block(TB, 0), pair_block(TB, 3), pair_block(TB, 0), pair_block(TB, 3),
        pair_block(TB), whole(8, KW), whole(TB, 1), whole(1, KW),
    ]


PARAMS = pltpu.CompilerParams(vmem_limit_bytes=48 * 1024 * 1024, dimension_semantics=("arbitrary",))


def attend(qkv, halo1, halo2, gate, decay, seg_q, seg_k):
    pairs = 3
    return pl.pallas_call(
        forward_kernel,
        grid=(pairs,),
        in_specs=attention_inputs(),
        out_specs=[pair_block(TB), pair_block(TB), per_pair(TB, 8)],
        out_shape=[
            jax.ShapeDtypeStruct((TB, pairs * 128), F32),
            jax.ShapeDtypeStruct((TB, pairs * 128), BF),
            jax.ShapeDtypeStruct((pairs, TB, 8), F32),
        ],
        scratch_shapes=[
            pltpu.VMEM((KW, 128), BF), pltpu.VMEM((KW, 128), BF),
            pltpu.VMEM((TB // CH, CH, SPAN), F32),
        ],
        compiler_params=PARAMS,
        cost_estimate=pl.CostEstimate(flops=2_400_000_000, bytes_accessed=8_000_000, transcendentals=4_000_000),
        name="attend",
    )(qkv, qkv, qkv, halo1, halo1, halo2, halo2, gate, decay, seg_q, seg_k)


def attend_back(qkv, halo1, halo2, grad_attended, decay, seg_q, seg_k, norm):
    pairs = 3
    return pl.pallas_call(
        backward_kernel,
        grid=(pairs,),
        in_specs=attention_inputs() + [per_pair(TB, 8)],
        out_specs=[
            pair_block(TB), pair_block(TB), pair_block(TB), whole(TB, 896), whole(TB, 896),
            whole(TB, EXT),
        ],
        out_shape=[
            jax.ShapeDtypeStruct((TB, pairs * 128), BF),
            jax.ShapeDtypeStruct((TB, pairs * 128), F32),
            jax.ShapeDtypeStruct((TB, pairs * 128), F32),
            jax.ShapeDtypeStruct((TB, 896), BF),
            jax.ShapeDtypeStruct((TB, 896), BF),
            jax.ShapeDtypeStruct((TB, EXT), F32),
        ],
        scratch_shapes=[
            pltpu.VMEM((KW, 128), BF), pltpu.VMEM((KW, 128), BF),
            pltpu.VMEM((TB // CH, CH, SPAN), F32),
            pltpu.VMEM((KW, 128), F32), pltpu.VMEM((KW, 128), F32),
            pltpu.VMEM((KW, EXT), F32), pltpu.VMEM((TB, EXT), F32),
        ],
        compiler_params=PARAMS,
        cost_estimate=pl.CostEstimate(flops=6_000_000_000, bytes_accessed=14_000_000, transcendentals=4_000_000),
        name="attend_back",
    )(qkv, qkv, qkv, halo1, halo1, halo2, halo2, grad_attended, decay, seg_q, seg_k, norm)


def one_hot(bases, j, features):
    at = lax.broadcasted_iota(jnp.int32, (WIDE, features.shape[1]), 0)
    piece = at + jnp.where(at < SHARD, bases[j], bases[PIECES + j] - SHARD)
    return (piece == features).astype(F32).astype(BF)


def arrange_kernel(*refs):
    bases, features = refs[0], refs[1]
    pieces = refs[2 : 2 + PIECES]
    source, normed, cot, gains, inverse, wide = refs[2 + PIECES :]

    @pl.when(pl.program_id(0) == 0)
    def _():
        total = jnp.zeros((TB, 1), F32)
        for j in range(PIECES):
            wide[:, j * WIDE : (j + 1) * WIDE] = pieces[j][...]
            rows = pieces[j][:TB, :].astype(F32)
            total = total + jnp.sum(rows * rows, axis=1, keepdims=True)
        inverse[...] = lax.rsqrt(total / D + EPS)

    hot = jnp.concatenate([one_hot(bases, j, features[...]) for j in range(PIECES)], axis=0)
    rows = dot(wide[TB:, :], hot)
    cot[...] = rows[:QUARTER].astype(BF)
    gains[...] = rows[QUARTER : QUARTER + 8]
    gain = rows[QUARTER : QUARTER + 1]
    for c in range(TB // CH):
        at = slice(c * CH, (c + 1) * CH)
        rows = dot(wide[at, :], hot)
        source[at, :] = rows.astype(BF)
        normed[at, :] = (rows * inverse[at, :] * gain).astype(BF)


def arrange(bases, features, pieces):
    def tile(rows):
        return pl.BlockSpec((rows, TILE), lambda n: (0, n))

    return pl.pallas_call(
        arrange_kernel,
        grid=(D // TILE,),
        in_specs=[pl.BlockSpec(memory_space=pltpu.SMEM), tile(1)] + [whole(ROWS_IN, WIDE)] * PIECES,
        out_specs=[tile(TB), tile(TB), tile(QUARTER), tile(8), whole(TB, 1)],
        out_shape=[
            jax.ShapeDtypeStruct((TB, D), BF),
            jax.ShapeDtypeStruct((TB, D), BF),
            jax.ShapeDtypeStruct((QUARTER, D), BF),
            jax.ShapeDtypeStruct((8, D), F32),
            jax.ShapeDtypeStruct((TB, 1), F32),
        ],
        scratch_shapes=[pltpu.VMEM((ROWS_IN, D), BF)],
        compiler_params=PARAMS,
        cost_estimate=pl.CostEstimate(flops=4_000_000_000, bytes_accessed=6_000_000, transcendentals=512),
        name="arrange",
    )(bases, features, *pieces)


def release_kernel(
    bases, features, partial, source, inverse, gain, grad_residual, output, piece, rows
):
    @pl.when(pl.program_id(0) == 0)
    def _():
        for c in range(GROUP_COLS):
            at = slice(c * QUARTER, (c + 1) * QUARTER)
            scaled = gain[...] * partial[at, :]
            values = source[at, :].astype(F32)
            scale = inverse[at, :]
            total = jnp.sum(scaled * values, axis=1, keepdims=True)
            part = scale * scaled - values * (scale * scale * scale * total / D)
            part = part + jnp.where(c == bases[2 * PIECES], grad_residual[...], 0.0)
            rows[at, :] = part.astype(BF)
        rows[TB:, :] = output[...]

    piece[0] = dot_t(rows[...], one_hot(bases, pl.program_id(0), features[...])).astype(BF)


def release(bases, features, partial, source, inverse, gain, grad_residual, output):
    return pl.pallas_call(
        release_kernel,
        grid=(PIECES,),
        in_specs=[
            pl.BlockSpec(memory_space=pltpu.SMEM), whole(1, D), whole(TB, D), whole(TB, D),
            whole(TB, 1), whole(1, D), whole(QUARTER, D), whole(QUARTER, D),
        ],
        out_specs=per_pair(ROWS_OUT, WIDE),
        out_shape=jax.ShapeDtypeStruct((PIECES, ROWS_OUT, WIDE), BF),
        scratch_shapes=[pltpu.VMEM((ROWS_OUT, D), BF)],
        compiler_params=PARAMS,
        cost_estimate=pl.CostEstimate(flops=4_000_000_000, bytes_accessed=8_000_000, transcendentals=512),
        name="release",
    )(bases, features, partial, source, inverse, gain, grad_residual, output)


def gather_x(both):
    return lax.all_gather(both, "x", axis=0, tiled=True)


def scatter_x(mine):
    return lax.psum_scatter(mine, "x", scatter_dimension=0, tiled=True)


def by_rows(matrix):
    return with_layout_constraint(matrix, Layout(major_to_minor=(0, 1)))


def with_partner(shard):
    return jnp.concatenate([shard, z_partner(shard)], axis=0)


def tie(*values):
    return lax.optimization_barrier(values)


def after(value, *others):
    return tie(value, *others)[0]


def leaving_rows(left, right):
    return t_dot(left[:, D // 2 :], right).astype(BF)


def summed_rows(left, right, arrived):
    return (t_dot(left[:, : D // 2], right) + arrived.astype(F32)).astype(BF)


def near_sum(part):
    rows = part.shape[0] // 2
    return part[:rows].astype(F32) + z_partner(part[rows:]).astype(F32)


def twin_sum(part):
    return rounded(part) + z_twin(rounded(part).astype(BF)).astype(F32)


def both_halves(part, other, core):
    part = rounded(part).astype(BF)
    return jnp.where(
        core == 0, jnp.concatenate([part, other], axis=0), jnp.concatenate([other, part], axis=0)
    ).astype(F32)


def reorder(pieces, key):
    return [lax.dynamic_index_in_dim(pieces, i ^ key, 0, keepdims=False) for i in range(pieces.shape[0])]


def body(
    block_input,
    attn_gain,
    attn_weight,
    forget_weight,
    forget_bias,
    out_weight,
    ffn_gain,
    gate_up_weight,
    down_weight,
    segments,
    cotangent,
):
    core = lax.axis_index("core")
    zh = lax.axis_index("zh")
    x = lax.axis_index("x")
    y = lax.axis_index("y")
    heads = forget_weight.shape[1]
    width = heads * HEAD_DIM
    ffn = down_weight.shape[0]
    shard = block_input.shape[1]
    half = shard // 2

    side = x % 2
    spot = 2 * zh + x // 2

    def half_rows(index):
        return [lax.dynamic_slice_in_dim(rows, index * TB, TB, 0) for rows in (block_input, cotangent)]

    gain_rows = jnp.pad(jnp.stack([attn_gain, ffn_gain]), ((0, 14), (0, 0)))
    far_rows = x_flip(jnp.concatenate(half_rows(1 - side) + [gain_rows], axis=0), 1)
    extra = jnp.pad(jnp.concatenate([forget_weight] * 3, axis=1), ((0, 0), (0, EXT - 3 * heads)))
    proj_cols = 4 * width + EXT

    def mine(rows):
        return lax.dynamic_slice_in_dim(rows, core * half, half, 0)

    first_both = with_partner(
        jnp.concatenate(
            [mine(attn_weight.reshape(shard, 4 * width)), mine(extra), mine(out_weight.T)], axis=1
        )
    )
    first_both = after(first_both, far_rows)
    wide_rows = jnp.concatenate(
        [jnp.concatenate(half_rows(side) + [gain_rows], axis=0), far_rows], axis=1
    )

    def leaving_tokens(step):
        return jnp.concatenate(
            [
                wide_rows[:TB],
                lax.dynamic_slice_in_dim(wide_rows, TB + (spot ^ step) * QUARTER, QUARTER, 0),
                wide_rows[2 * TB :],
            ]
        )

    arrived = [lax.ppermute(leaving_tokens(j), ALL, to_groups(j)) for j in range(PIECES)]

    first_half = gather_x(first_both)
    ffn_both = with_partner(
        jnp.concatenate(
            [mine(gate_up_weight.reshape(shard, 2 * ffn)), mine(down_weight.T)], axis=1
        )
    )
    other_segments = core_flip(segments)

    col_at = jnp.arange(D, dtype=jnp.int32)
    block = col_at // half
    features = (
        ((zh ^ (block % 2)) * 4 + (block // 2) % 4) * shard
        + (core ^ (block // 8)) * half + col_at % half
    )[None, :]
    spots = jnp.arange(PIECES, dtype=jnp.int32) ^ y
    rows_x = (spots // 2) * 4 + 2 * (spots % 2)
    bases = jnp.concatenate(
        [(rows_x + side) * shard, (rows_x + 1 - side) * shard, y[None].astype(jnp.int32)]
    )
    source_low, normed, cot_mine, gains, inverse_first = arrange(bases, features, arrived)
    gain_first, gain_second = gains[0:1], gains[1:2]
    first_half, ffn_both, other_segments, normed = tie(
        first_half, ffn_both, other_segments, normed
    )

    first_other = core_flip(first_half)
    w_proj = jnp.concatenate([first_half, first_other], axis=0)
    out_half = first_half[:, proj_cols:]
    out_others = [y_flip(out_half, d) for d in range(1, 4)]
    projected = dot(normed[:, : D // 2], first_half) + dot(normed[:, D // 2 :], first_other)
    qkv = projected[:, : 3 * width].astype(BF)
    lanes = lax.broadcasted_iota(jnp.int32, (1, EXT), 1)
    earlier = (
        lax.broadcasted_iota(jnp.int32, (TB, TB), 0) >= lax.broadcasted_iota(jnp.int32, (TB, TB), 1)
    ).astype(F32)
    bias_lanes = jnp.pad(jnp.concatenate([forget_bias] * 3), (0, EXT - 3 * heads))[None, :]
    gate_logit = projected[:, 3 * width : 4 * width]
    forget_lanes = projected[:, 4 * width : proj_cols] + bias_lanes
    cumulative = jnp.dot(earlier, jax.nn.log_sigmoid(forget_lanes), precision=HIGHEST)
    rest = cumulative - rounded(cumulative)
    parts = jnp.where(
        lanes < heads, cumulative, jnp.where(lanes < 2 * heads, rest, rest - rounded(rest))
    ).astype(BF)

    sequence_block = 2 * core + x % 2
    key_values = jnp.concatenate([qkv[:, width:], parts], axis=1)
    halo1 = block_shift(key_values, 1)
    halo2 = block_shift(key_values, 2)
    cot_leaving = after(cot_mine, key_values)
    cot_others = [y_flip(cot_leaving, d) for d in range(1, 4)]
    own = jnp.where(x // 2 == core, segments, other_segments)
    own = lax.dynamic_index_in_dim(own, zh, 0, keepdims=False)
    padded = jnp.concatenate([jnp.full((2 * TB,), -1, jnp.int32), own])
    seg_k = lax.dynamic_slice_in_dim(padded, sequence_block * TB, KW)
    seg_q = lax.dynamic_slice_in_dim(own, sequence_block * TB, TB)[:, None]
    seg_k = seg_k[None, :]
    out_half = jnp.concatenate([out_half] + out_others, axis=1)
    halo1, halo2, qkv, gate_logit, seg_q, seg_k, out_half = tie(
        halo1, halo2, qkv, gate_logit, seg_q, seg_k, out_half
    )
    out_other = core_flip(out_half)
    ffn_half = gather_x(after(ffn_both, halo1))
    column = lax.broadcasted_iota(jnp.int32, (EXT, 8), 1)
    lane_at = lax.broadcasted_iota(jnp.int32, (EXT, 8), 0)
    gather_parts = ((lane_at % heads == column) & (lane_at < 3 * heads)).astype(BF)
    decay = lax.dot_general(
        gather_parts,
        jnp.concatenate([halo2[:, 2 * width :], halo1[:, 2 * width :], parts], axis=0),
        (((0,), (1,)), ((), ())),
        preferred_element_type=F32,
    )
    last1 = decay[:, 2 * TB - 1 : 2 * TB]
    last2 = decay[:, TB - 1 : TB] + last1
    key_at = lax.broadcasted_iota(jnp.int32, (1, KW), 1)
    decay = decay - jnp.where(key_at < TB, last2, jnp.where(key_at < 2 * TB, last1, 0.0))
    attended, gated, norm = attend(qkv, halo1, halo2, gate_logit, decay, seg_q, seg_k)
    gated, out_other, *cot_others = tie(gated, out_other, *cot_others)
    gated_others = [y_flip(gated, d) for d in range(1, 4)]
    w_out = tie(jnp.concatenate([out_half, out_other], axis=0))[0]
    ffn_half = after(ffn_half, *gated_others)
    w_ffn = jnp.concatenate([ffn_half, core_flip(ffn_half)], axis=0)
    w_gate_up, w_down = w_ffn[:, : 2 * ffn], w_ffn[:, 2 * ffn :]
    cot = jnp.concatenate(reorder(jnp.stack([cot_mine] + cot_others), y), axis=0)

    gated_all = jnp.concatenate([gated] + gated_others, axis=1)
    residual = source_low.astype(F32) + dot_t(gated_all, w_out)
    inverse_second = lax.rsqrt(jnp.mean(residual * residual, axis=1, keepdims=True) + EPS)
    normed_second = (residual * inverse_second * gain_second).astype(BF)
    gate_up = dot(normed_second, w_gate_up)
    gate_rows, up_rows = gate_up[:, :ffn], gate_up[:, ffn:]
    ffn_open = jax.nn.sigmoid(gate_rows)
    hidden = (gate_rows * ffn_open * up_rows).astype(BF)
    grad_hidden = dot(cot, w_down)
    grad_gate_up = jnp.concatenate(
        [
            (grad_hidden * up_rows * ffn_open * (1.0 + gate_rows * (1.0 - ffn_open))).astype(BF),
            (grad_hidden * gate_rows * ffn_open).astype(BF),
        ],
        axis=1,
    )

    def rows_of(matrix, index):
        return lax.dynamic_slice_in_dim(matrix, index * QUARTER, QUARTER, 0)

    def others_rows(partial):
        return [y_flip(rows_of(partial, y ^ d).astype(BF), d) for d in range(1, 4)]

    def summed(first, others):
        return first + sum(other.astype(F32) for other in others)

    partial_second = dot_t(grad_gate_up, w_gate_up)
    second_others = others_rows(partial_second)
    second_mine = rows_of(partial_second, y)

    gate_up_arrived = core_flip(leaving_rows(normed_second, grad_gate_up))
    down_arrived = core_flip(leaving_rows(cot, hidden))
    gate_up_mine = summed_rows(normed_second, grad_gate_up, gate_up_arrived)
    down_mine = summed_rows(cot, hidden, down_arrived)
    ffn_mine, *second_others = tie(
        jnp.concatenate([gate_up_mine, down_mine], axis=1), *second_others
    )
    ffn_scattered = scatter_x(ffn_mine)
    output_partial = dot_t(hidden, w_down)
    output_mine = rows_of(output_partial, y)
    output_leaving = [rows_of(output_partial, y ^ d).astype(BF) for d in range(1, 4)]
    second_others[0], output_mine, *output_leaving = tie(
        second_others[0], output_mine, *output_leaving
    )
    grad_normed_second = summed(second_mine, second_others)
    residual_mine = rows_of(residual, y)
    inverse_mine = rows_of(inverse_second, y)
    scaled = gain_second * grad_normed_second
    second_dot = jnp.sum(scaled * residual_mine, axis=1, keepdims=True)
    grad_residual = (
        cot_mine.astype(F32)
        + inverse_mine * scaled
        - residual_mine * (inverse_mine**3 * second_dot / D)
    )
    grad_branch = grad_residual.astype(BF)
    grad_gated_all = dot(grad_branch, w_out).astype(BF)
    gated_pieces = jnp.stack(
        [grad_gated_all[:, :width]]
        + [y_flip(grad_gated_all[:, d * width : (d + 1) * width], d) for d in range(1, 4)]
    )
    grad_gated = jnp.concatenate(reorder(gated_pieces, y), axis=0).astype(F32)
    grad_gated, grad_branch = tie(grad_gated, grad_branch)
    branch_others = [y_flip(grad_branch, d) for d in range(1, 4)]

    gate_open = jax.nn.sigmoid(gate_logit)
    grad_attended = (grad_gated * gate_open).astype(BF)
    dgate = (grad_gated * attended * gate_open * (1.0 - gate_open)).astype(BF)
    dq, dk, dv, d1, d2, forget_part = attend_back(
        qkv, halo1, halo2, grad_attended, decay, seg_q, seg_k, norm
    )
    d1, d2, dgate, ffn_scattered, *others = tie(
        d1, d2, dgate, ffn_scattered, *output_leaving, *branch_others
    )
    output_leaving, branch_others = others[:3], others[3:]
    back1 = block_shift(d1, -1)
    back2 = block_shift(d2, -2)
    output_others = [y_flip(output_leaving[d - 1], d) for d in range(1, 4)]

    grad_branch, dgate, dq, *branch_others = tie(grad_branch, dgate, dq, *branch_others, back2)[:-1]
    partial_early = dot_t(dq, w_proj[:, :width]) + dot_t(dgate, w_proj[:, 3 * width : 4 * width])
    branch_rows = jnp.concatenate([grad_branch] + branch_others, axis=0)
    gated_rows = jnp.concatenate([rows_of(gated, y ^ d) for d in range(4)], axis=0)
    sooner = jnp.concatenate([dgate, dq], axis=1)
    sooner_leaving = jnp.concatenate(
        [leaving_rows(branch_rows, gated_rows), leaving_rows(normed, sooner)], axis=1
    )
    ffn_near = near_sum(after(ffn_scattered, back2))
    back1, back2, ffn_near, sooner_leaving, *output_others = tie(
        back1, back2, ffn_near, sooner_leaving, *output_others
    )
    ffn_part = twin_sum(ffn_near)
    back1, back2 = back1.astype(F32), back2.astype(F32)
    key_sums = back1[:, : 2 * width] + back2[:, : 2 * width]
    output_mine = (residual_mine + summed(output_mine, output_others)).astype(BF)

    from_lane = lax.broadcasted_iota(jnp.int32, (EXT, 1), 0)
    same_head = (from_lane % heads == lanes % heads) & (lanes < 2 * heads)
    join = (same_head & (from_lane < 2 * heads)).astype(F32)
    join_far = (same_head & (from_lane >= 2 * heads) & (from_lane < 4 * heads)).astype(F32)
    sums1, sums2 = back1[:, 2 * width :], back2[:, 2 * width :]
    other_sums = jnp.dot(sums1 + sums2, join, precision=HIGHEST)
    later = jnp.sum(other_sums, axis=0, keepdims=True) + jnp.dot(
        sums1[:1], join_far, precision=HIGHEST
    )
    suffix = lax.dot_general(
        earlier, forget_part - other_sums, (((0,), (0,)), ((), ())), precision=HIGHEST
    ) + later
    grad_forget = suffix * jax.nn.sigmoid(-forget_lanes)
    grad_extra = jnp.where(
        lanes < heads, grad_forget, jnp.where(lanes < 2 * heads, grad_forget - rounded(grad_forget), 0.0)
    ).astype(BF)
    dk_all = (dk + key_sums[:, :width]).astype(BF)
    dv_all = (dv + key_sums[:, width:]).astype(BF)

    late = jnp.concatenate([dk_all, dv_all, grad_extra], axis=1)
    leaving_late = leaving_rows(normed, late)
    attn_arrived = core_flip(by_rows(jnp.concatenate([sooner_leaving, leaving_late], axis=1)))
    early_cols = 3 * width
    attn_mine = jnp.concatenate(
        [
            summed_rows(branch_rows, gated_rows, attn_arrived[:, :width]),
            summed_rows(normed, sooner, attn_arrived[:, width:early_cols]),
            summed_rows(normed, late, attn_arrived[:, early_cols:]),
        ],
        axis=1,
    )
    attn_mine = by_rows(attn_mine)
    attn_scattered = scatter_x(attn_mine)
    late = after(late, attn_mine)
    partial_first = (
        partial_early
        + dot_t(late[:, : 2 * width], w_proj[:, width : 3 * width])
        + dot_t(late[:, 2 * width :], w_proj[:, 4 * width : proj_cols])
    )

    leaving = release(
        bases, features, partial_first, source_low, inverse_first, gain_first, grad_residual, output_mine
    )
    ffn_other = core_flip(rounded(ffn_part).astype(BF))
    leaving, ffn_part = tie(leaving, ffn_part)
    returned = [lax.ppermute(leaving[j], ALL, from_groups(j)) for j in range(PIECES)]
    bias_sum = after(
        jnp.broadcast_to(jnp.sum(grad_forget, axis=0, keepdims=True), (8, EXT)), leaving
    )
    for other in (core_flip, lambda v: x_flip(v, 1), lambda v: x_flip(v, 2), z_partner, z_twin):
        bias_sum = bias_sum + other(bias_sum)
    attn_part = twin_sum(near_sum(attn_scattered))
    bias_sum, *returned = tie(bias_sum, *returned)
    input_rows = sum(piece[:TB].astype(F32) for piece in returned)
    output_rows = jnp.concatenate(reorder(jnp.stack([piece[TB:] for piece in returned]), spot), axis=0)
    far_rows = x_flip(
        jnp.concatenate([input_rows[:, shard:].astype(BF), output_rows[:, shard:]], axis=0), 1
    )
    near, far = input_rows[:, :shard], far_rows[:TB].astype(F32)
    input_grad = jnp.concatenate(
        [jnp.where(side == 0, near, far), jnp.where(side == 0, far, near)], axis=0
    )
    near, far = output_rows[:, :shard], far_rows[TB:]
    block_output = jnp.concatenate(
        [jnp.where(side == 0, near, far), jnp.where(side == 0, far, near)], axis=0
    )

    ffn_full = both_halves(ffn_part, ffn_other, core)
    attn_other = core_flip(rounded(attn_part).astype(BF))
    attn_all = both_halves(attn_part, attn_other, core)
    attn_part = after(attn_part, attn_other)
    extras = attn_all[:, 5 * width :]
    forget_grad = extras[:, :heads] + extras[:, heads : 2 * heads]
    attn_full = jnp.concatenate(
        [attn_all[:, 2 * width : 5 * width], attn_all[:, width : 2 * width]], axis=1
    )

    def row_dot(weight, grad):
        return jnp.sum(mine(weight).astype(F32) * grad, axis=1)

    gain_parts = jnp.stack(
        [
            (
                row_dot(attn_weight[:, :3].reshape(shard, 3 * width), attn_part[:, 2 * width : 5 * width])
                + row_dot(attn_weight[:, 3], attn_part[:, width : 2 * width])
                + row_dot(
                    jnp.concatenate([forget_weight] * 2, axis=1),
                    attn_part[:, 5 * width : 5 * width + 2 * heads],
                )
            )
            / mine(attn_gain).astype(F32),
            row_dot(gate_up_weight.reshape(shard, 2 * ffn), ffn_part[:, : 2 * ffn])
            / mine(ffn_gain).astype(F32),
        ]
    )
    gain_others = [y_flip(gain_parts, d) for d in range(1, 4)]
    gain_half = (gain_parts + gain_others[0]) + (gain_others[1] + gain_others[2])
    gain_other = core_flip(gain_half)
    gain_sum = jnp.where(
        core == 0,
        jnp.concatenate([gain_half, gain_other], axis=1),
        jnp.concatenate([gain_other, gain_half], axis=1),
    )
    return (
        block_output,
        input_grad,
        gain_sum[0],
        attn_full.reshape(attn_weight.shape),
        forget_grad,
        bias_sum[0, :heads],
        attn_all[:, :width].T,
        gain_sum[1],
        ffn_full[:, : 2 * ffn].reshape(gate_up_weight.shape),
        ffn_full[:, 2 * ffn :].T,
    )


def solution(mesh):
    inner = Mesh(mesh.devices.reshape(DIMS), ALL)
    dp, row = ("zl", "core"), ("zh", "x")
    tokens = P(("zl", "core", "y"), row)
    in_specs = (
        tokens, P(row), P(row, None, "y"), P(row, "y"), P("y"), P("y", row), P(row),
        P(row, None, "y"), P("y", row), P(dp, None), tokens,
    )
    out_specs = (
        tokens, tokens, P(row), P(row, None, "y"), P(row, "y"), P("y"), P("y", row), P(row),
        P(row, None, "y"), P("y", row),
    )
    return jax.shard_map(body, mesh=inner, in_specs=in_specs, out_specs=out_specs, check_vma=False)
```

```python
import jax
import jax.numpy as jnp
from jax import lax
from jax.experimental import pallas as pl
from jax.experimental.layout import Layout, with_layout_constraint
from jax.experimental.pallas import tpu as pltpu
from jax.sharding import Mesh, PartitionSpec as P

D = 1536
HEAD_DIM = 64
WINDOW = 1024
EPS = 1e-06
MASKED = -1e30
ALL = ("zl", "core", "zh", "x", "y")
DIMS = (2, 2, 2, 4, 4)
BF = jnp.bfloat16
F32 = jnp.float32
HIGHEST = lax.Precision.HIGHEST

TB = 512
KW = 3 * TB
CH = 256
SPAN = WINDOW + CH
GROUP_COLS = 4
EXT = 128
HEADS_COL = 6
PIECES = 4
SHARD = D // 8
WIDE = 2 * SHARD
QUARTER = TB // GROUP_COLS
ROWS_IN = TB + QUARTER + 16
ROWS_OUT = TB + QUARTER
TILE = 256


def place(zl, core, zh, x, y):
    return (((zl * 2 + core) * 2 + zh) * 4 + x) * 4 + y


def places():
    for zl in range(2):
        for core in range(2):
            for zh in range(2):
                for x in range(4):
                    for y in range(4):
                        yield zl, core, zh, x, y


def to_groups(step):
    return [
        (
            place(zl, core, zh, x, y),
            place(zl, y % 2, y // 2, 2 * core + x % 2, (2 * zh + x // 2) ^ step),
        )
        for zl, core, zh, x, y in places()
    ]


def from_groups(step):
    return [(target, source) for source, target in to_groups(step)]


def flip(value, axis, size, bits):
    return lax.ppermute(value, axis, [(i, i ^ bits) for i in range(size)])


def core_flip(value):
    return flip(value, "core", 2, 1)


def z_partner(value):
    return flip(value, ("zl", "zh"), 4, 3)


def zh_flip(value):
    return flip(value, "zh", 2, 1)


def z_twin(value):
    return flip(value, "zl", 2, 1)


def x_flip(value, bits):
    return flip(value, "x", 4, bits)


def y_flip(value, bits):
    return flip(value, "y", 4, bits)


def block_shift(value, distance):
    pairs = []
    for core in range(2):
        for x in range(4):
            block = 2 * core + x % 2
            other = block + distance
            if 0 <= other < 4:
                pairs.append((core * 4 + x, (other // 2) * 4 + (x // 2) * 2 + other % 2))
    return lax.ppermute(value, ("core", "x"), pairs)


def dot(a, b):
    return lax.dot_general(a, b, (((1,), (0,)), ((), ())), preferred_element_type=F32)


def dot_t(a, b):
    return lax.dot_general(a, b, (((1,), (1,)), ((), ())), preferred_element_type=F32)


def t_dot(a, b):
    return lax.dot_general(a, b, (((0,), (0,)), ((), ())), preferred_element_type=F32)


def rounded(value):
    return lax.reduce_precision(value, exponent_bits=8, mantissa_bits=7)


def head_lanes(head):
    lanes = lax.broadcasted_iota(jnp.int32, (1, 2 * HEAD_DIM), 1)
    return (lanes >= HEAD_DIM) if head else (lanes < HEAD_DIM)


def fill_mask(mask, seg_q, seg_k):
    for c in range(TB // CH):
        rows = lax.broadcasted_iota(jnp.int32, (CH, SPAN), 0)
        cols = lax.broadcasted_iota(jnp.int32, (CH, SPAN), 1)
        gap = rows + WINDOW - cols
        same = seg_q[c * CH : (c + 1) * CH, :] == seg_k[:, c * CH : c * CH + SPAN]
        keep = (gap >= 0) & (gap < WINDOW) & same
        mask[c] = jnp.where(keep, 0.0, MASKED)


def forward_kernel(
    q, k, v, k1, v1, k2, v2, gate, decay, seg_q, seg_k, att, gated, norm, keys, values, mask
):
    pair = pl.program_id(0)

    @pl.when(pair == 0)
    def _():
        fill_mask(mask, seg_q, seg_k)

    keys[0:TB, :] = k2[...]
    keys[TB : 2 * TB, :] = k1[...]
    keys[2 * TB :, :] = k[...]
    values[0:TB, :] = v2[...]
    values[TB : 2 * TB, :] = v1[...]
    values[2 * TB :, :] = v[...]
    lane = lax.broadcasted_iota(jnp.int32, (CH, 8), 1)
    for c in range(TB // CH):
        rows = slice(c * CH, (c + 1) * CH)
        span = slice(c * CH, c * CH + SPAN)
        mixed, norms = [], []
        for h in range(2):
            mine = head_lanes(h)
            q_h = jnp.where(mine, q[rows, :], jnp.zeros((), BF)) * jnp.asarray(HEAD_DIM**-0.5, BF)
            s = dot_t(q_h, keys[span, :]) - decay[pl.ds(2 * pair + h, 1), span] + mask[c]
            top = jnp.max(s, axis=1, keepdims=True)
            e = jnp.exp(s - top)
            total = jnp.sum(e, axis=1, keepdims=True)
            p = (e * (1.0 / total)).astype(BF)
            mixed.append(dot(p, values[span, :]))
            norms.append(top + jnp.log(total))
        out = jnp.where(head_lanes(0), mixed[0], mixed[1])
        att[rows, :] = out
        gated[rows, :] = (out * jax.nn.sigmoid(gate[rows, :])).astype(BF)
        norm[0, rows, :] = jnp.where(lane == 0, norms[0], norms[1])


def backward_kernel(
    q, k, v, k1, v1, k2, v2, grad_attended, decay, seg_q, seg_k, norm,
    dq, dk, dv, d1, d2, forget,
    keys, values, mask, dk_sum, dv_sum, col_sum, row_sum,
):
    pair = pl.program_id(0)
    lane = lax.broadcasted_iota(jnp.int32, (1, EXT), 1)

    @pl.when(pair == 0)
    def _():
        fill_mask(mask, seg_q, seg_k)
        col_sum[...] = jnp.zeros_like(col_sum)
        row_sum[...] = jnp.zeros_like(row_sum)

    keys[0:TB, :] = k2[...]
    keys[TB : 2 * TB, :] = k1[...]
    keys[2 * TB :, :] = k[...]
    values[0:TB, :] = v2[...]
    values[TB : 2 * TB, :] = v1[...]
    values[2 * TB :, :] = v[...]
    dk_sum[...] = jnp.zeros_like(dk_sum)
    dv_sum[...] = jnp.zeros_like(dv_sum)
    for c in range(TB // CH):
        rows = slice(c * CH, (c + 1) * CH)
        span = slice(c * CH, c * CH + SPAN)
        grad = grad_attended[rows, :]
        dq_parts = []
        for h in range(2):
            mine = head_lanes(h)
            marks = ((lane % HEADS_COL == 2 * pair + h) & (lane < 4 * HEADS_COL)).astype(F32)
            q_h = jnp.where(mine, q[rows, :], jnp.zeros((), BF)) * jnp.asarray(HEAD_DIM**-0.5, BF)
            g_h = jnp.where(mine, grad, jnp.zeros((), BF))
            s = dot_t(q_h, keys[span, :]) - decay[pl.ds(2 * pair + h, 1), span] + mask[c]
            p = jnp.exp(s - norm[0, rows, h : h + 1])
            dp = dot_t(g_h, values[span, :])
            total = jnp.sum(p * dp, axis=1, keepdims=True)
            ds = (p * (dp - total)).astype(BF)
            dq_parts.append(dot(ds, keys[span, :]))
            wide = t_dot(
                ds, jnp.concatenate([q_h, jnp.broadcast_to(marks, (CH, EXT)).astype(BF)], axis=1)
            )
            dk_sum[span, :] += wide[:, :128]
            col_sum[span, :] += wide[:, 128:]
            dv_sum[span, :] += t_dot(p.astype(BF), g_h)
            row_sum[rows, :] += jnp.sum(ds.astype(F32), axis=1, keepdims=True) * marks
        dq[rows, :] = (jnp.where(head_lanes(0), dq_parts[0], dq_parts[1]) * HEAD_DIM**-0.5).astype(BF)
    k_at = pl.ds(pl.multiple_of(pair * 128, 128), 128)
    v_at = pl.ds(pl.multiple_of(384 + pair * 128, 128), 128)
    d2[:, k_at] = dk_sum[0:TB, :].astype(BF)
    d2[:, v_at] = dv_sum[0:TB, :].astype(BF)
    d1[:, k_at] = dk_sum[TB : 2 * TB, :].astype(BF)
    d1[:, v_at] = dv_sum[TB : 2 * TB, :].astype(BF)
    dk[...] = dk_sum[2 * TB :, :]
    dv[...] = dv_sum[2 * TB :, :]

    @pl.when(pair == pl.num_programs(0) - 1)
    def _():
        forget[...] = row_sum[...] - col_sum[2 * TB :, :]

        def parts(value):
            high = value.astype(BF).astype(F32)
            return jnp.where((lane // HEADS_COL) % 2 == 0, high, value - high)

        far, near = col_sum[0:TB, :], col_sum[TB : 2 * TB, :]
        all_far = jnp.sum(far, axis=0, keepdims=True)
        d2[:, 768:] = jnp.where(lane < 2 * HEADS_COL, parts(far), 0.0).astype(BF)
        d1[:, 768:] = jnp.where(lane < 2 * HEADS_COL, parts(near), parts(all_far)).astype(BF)


def pair_block(rows, offset=0):
    return pl.BlockSpec((rows, 128), lambda p, offset=offset: (0, p + offset))


def whole(*shape):
    return pl.BlockSpec(shape, lambda p: (0,) * len(shape))


def per_pair(*shape):
    return pl.BlockSpec((1,) + shape, lambda p: (p,) + (0,) * len(shape))


def attention_inputs():
    return [
        pair_block(TB, 0), pair_block(TB, 3), pair_block(TB, 6),
        pair_block(TB, 0), pair_block(TB, 3), pair_block(TB, 0), pair_block(TB, 3),
        pair_block(TB), whole(8, KW), whole(TB, 1), whole(1, KW),
    ]


PARAMS = pltpu.CompilerParams(vmem_limit_bytes=48 * 1024 * 1024, dimension_semantics=("arbitrary",))


def attend(qkv, halo1, halo2, gate, decay, seg_q, seg_k):
    pairs = 3
    return pl.pallas_call(
        forward_kernel,
        grid=(pairs,),
        in_specs=attention_inputs(),
        out_specs=[pair_block(TB), pair_block(TB), per_pair(TB, 8)],
        out_shape=[
            jax.ShapeDtypeStruct((TB, pairs * 128), F32),
            jax.ShapeDtypeStruct((TB, pairs * 128), BF),
            jax.ShapeDtypeStruct((pairs, TB, 8), F32),
        ],
        scratch_shapes=[
            pltpu.VMEM((KW, 128), BF), pltpu.VMEM((KW, 128), BF),
            pltpu.VMEM((TB // CH, CH, SPAN), F32),
        ],
        compiler_params=PARAMS,
        cost_estimate=pl.CostEstimate(flops=2_400_000_000, bytes_accessed=8_000_000, transcendentals=4_000_000),
        name="attend",
    )(qkv, qkv, qkv, halo1, halo1, halo2, halo2, gate, decay, seg_q, seg_k)


def attend_back(qkv, halo1, halo2, grad_attended, decay, seg_q, seg_k, norm):
    pairs = 3
    return pl.pallas_call(
        backward_kernel,
        grid=(pairs,),
        in_specs=attention_inputs() + [per_pair(TB, 8)],
        out_specs=[
            pair_block(TB), pair_block(TB), pair_block(TB), whole(TB, 896), whole(TB, 896),
            whole(TB, EXT),
        ],
        out_shape=[
            jax.ShapeDtypeStruct((TB, pairs * 128), BF),
            jax.ShapeDtypeStruct((TB, pairs * 128), F32),
            jax.ShapeDtypeStruct((TB, pairs * 128), F32),
            jax.ShapeDtypeStruct((TB, 896), BF),
            jax.ShapeDtypeStruct((TB, 896), BF),
            jax.ShapeDtypeStruct((TB, EXT), F32),
        ],
        scratch_shapes=[
            pltpu.VMEM((KW, 128), BF), pltpu.VMEM((KW, 128), BF),
            pltpu.VMEM((TB // CH, CH, SPAN), F32),
            pltpu.VMEM((KW, 128), F32), pltpu.VMEM((KW, 128), F32),
            pltpu.VMEM((KW, EXT), F32), pltpu.VMEM((TB, EXT), F32),
        ],
        compiler_params=PARAMS,
        cost_estimate=pl.CostEstimate(flops=6_000_000_000, bytes_accessed=14_000_000, transcendentals=4_000_000),
        name="attend_back",
    )(qkv, qkv, qkv, halo1, halo1, halo2, halo2, grad_attended, decay, seg_q, seg_k, norm)


def one_hot(bases, j, features):
    at = lax.broadcasted_iota(jnp.int32, (WIDE, features.shape[1]), 0)
    piece = at + jnp.where(at < SHARD, bases[j], bases[PIECES + j] - SHARD)
    return (piece == features).astype(F32).astype(BF)


def arrange_kernel(*refs):
    bases, features = refs[0], refs[1]
    pieces = refs[2 : 2 + PIECES]
    source, normed, cot, gains, inverse, wide = refs[2 + PIECES :]

    @pl.when(pl.program_id(0) == 0)
    def _():
        total = jnp.zeros((TB, 1), F32)
        for j in range(PIECES):
            wide[:, j * WIDE : (j + 1) * WIDE] = pieces[j][...]
            rows = pieces[j][:TB, :].astype(F32)
            total = total + jnp.sum(rows * rows, axis=1, keepdims=True)
        inverse[...] = lax.rsqrt(total / D + EPS)

    hot = jnp.concatenate([one_hot(bases, j, features[...]) for j in range(PIECES)], axis=0)
    rows = dot(wide[TB:, :], hot)
    cot[...] = rows[:QUARTER].astype(BF)
    gains[...] = rows[QUARTER : QUARTER + 8]
    gain = rows[QUARTER : QUARTER + 1]
    for c in range(TB // CH):
        at = slice(c * CH, (c + 1) * CH)
        rows = dot(wide[at, :], hot)
        source[at, :] = rows.astype(BF)
        normed[at, :] = (rows * inverse[at, :] * gain).astype(BF)


def arrange(bases, features, pieces):
    def tile(rows):
        return pl.BlockSpec((rows, TILE), lambda n: (0, n))

    return pl.pallas_call(
        arrange_kernel,
        grid=(D // TILE,),
        in_specs=[pl.BlockSpec(memory_space=pltpu.SMEM), tile(1)] + [whole(ROWS_IN, WIDE)] * PIECES,
        out_specs=[tile(TB), tile(TB), tile(QUARTER), tile(8), whole(TB, 1)],
        out_shape=[
            jax.ShapeDtypeStruct((TB, D), BF),
            jax.ShapeDtypeStruct((TB, D), BF),
            jax.ShapeDtypeStruct((QUARTER, D), BF),
            jax.ShapeDtypeStruct((8, D), F32),
            jax.ShapeDtypeStruct((TB, 1), F32),
        ],
        scratch_shapes=[pltpu.VMEM((ROWS_IN, D), BF)],
        compiler_params=PARAMS,
        cost_estimate=pl.CostEstimate(flops=4_000_000_000, bytes_accessed=6_000_000, transcendentals=512),
        name="arrange",
    )(bases, features, *pieces)


def release_kernel(
    bases, features, partial, source, inverse, gain, grad_residual, output, piece, rows
):
    @pl.when(pl.program_id(0) == 0)
    def _():
        for c in range(GROUP_COLS):
            at = slice(c * QUARTER, (c + 1) * QUARTER)
            scaled = gain[...] * partial[at, :]
            values = source[at, :].astype(F32)
            scale = inverse[at, :]
            total = jnp.sum(scaled * values, axis=1, keepdims=True)
            part = scale * scaled - values * (scale * scale * scale * total / D)
            part = part + jnp.where(c == bases[2 * PIECES], grad_residual[...], 0.0)
            rows[at, :] = part.astype(BF)
        rows[TB:, :] = output[...]

    piece[0] = dot_t(rows[...], one_hot(bases, pl.program_id(0), features[...])).astype(BF)


def release(bases, features, partial, source, inverse, gain, grad_residual, output):
    return pl.pallas_call(
        release_kernel,
        grid=(PIECES,),
        in_specs=[
            pl.BlockSpec(memory_space=pltpu.SMEM), whole(1, D), whole(TB, D), whole(TB, D),
            whole(TB, 1), whole(1, D), whole(QUARTER, D), whole(QUARTER, D),
        ],
        out_specs=per_pair(ROWS_OUT, WIDE),
        out_shape=jax.ShapeDtypeStruct((PIECES, ROWS_OUT, WIDE), BF),
        scratch_shapes=[pltpu.VMEM((ROWS_OUT, D), BF)],
        compiler_params=PARAMS,
        cost_estimate=pl.CostEstimate(flops=4_000_000_000, bytes_accessed=8_000_000, transcendentals=512),
        name="release",
    )(bases, features, partial, source, inverse, gain, grad_residual, output)


def gather_x(both):
    return lax.all_gather(both, "x", axis=0, tiled=True)


def scatter_x(mine):
    return lax.psum_scatter(mine, "x", scatter_dimension=0, tiled=True)


def by_rows(matrix):
    return with_layout_constraint(matrix, Layout(major_to_minor=(0, 1)))


def with_partner(shard):
    return jnp.concatenate([shard, z_partner(shard)], axis=0)


def tie(*values):
    return lax.optimization_barrier(values)


def after(value, *others):
    return tie(value, *others)[0]


def leaving_rows(left, right):
    return t_dot(left[:, D // 2 :], right).astype(BF)


def summed_rows(left, right, arrived):
    return (t_dot(left[:, : D // 2], right) + arrived.astype(F32)).astype(BF)


def near_sum(part):
    rows = part.shape[0] // 2
    return part[:rows].astype(F32) + z_partner(part[rows:]).astype(F32)


def twin_sum(part):
    return rounded(part) + z_twin(rounded(part).astype(BF)).astype(F32)


def both_halves(part, other, core):
    part = rounded(part).astype(BF)
    return jnp.where(
        core == 0, jnp.concatenate([part, other], axis=0), jnp.concatenate([other, part], axis=0)
    ).astype(F32)


def reorder(pieces, key):
    return [lax.dynamic_index_in_dim(pieces, i ^ key, 0, keepdims=False) for i in range(pieces.shape[0])]


def body(
    block_input,
    attn_gain,
    attn_weight,
    forget_weight,
    forget_bias,
    out_weight,
    ffn_gain,
    gate_up_weight,
    down_weight,
    segments,
    cotangent,
):
    core = lax.axis_index("core")
    zh = lax.axis_index("zh")
    x = lax.axis_index("x")
    y = lax.axis_index("y")
    heads = forget_weight.shape[1]
    width = heads * HEAD_DIM
    ffn = down_weight.shape[0]
    shard = block_input.shape[1]
    half = shard // 2

    side = x % 2
    spot = 2 * zh + x // 2

    def half_rows(index):
        return [lax.dynamic_slice_in_dim(rows, index * TB, TB, 0) for rows in (block_input, cotangent)]

    gain_rows = jnp.pad(jnp.stack([attn_gain, ffn_gain]), ((0, 14), (0, 0)))
    far_rows = x_flip(jnp.concatenate(half_rows(1 - side) + [gain_rows], axis=0), 1)
    extra = jnp.pad(jnp.concatenate([forget_weight] * 3, axis=1), ((0, 0), (0, EXT - 3 * heads)))
    proj_cols = 4 * width + EXT

    def mine(rows):
        return lax.dynamic_slice_in_dim(rows, core * half, half, 0)

    first_both = with_partner(
        jnp.concatenate(
            [mine(attn_weight.reshape(shard, 4 * width)), mine(extra), mine(out_weight.T)], axis=1
        )
    )
    first_both = after(first_both, far_rows)
    wide_rows = jnp.concatenate(
        [jnp.concatenate(half_rows(side) + [gain_rows], axis=0), far_rows], axis=1
    )

    def leaving_tokens(step):
        return jnp.concatenate(
            [
                wide_rows[:TB],
                lax.dynamic_slice_in_dim(wide_rows, TB + (spot ^ step) * QUARTER, QUARTER, 0),
                wide_rows[2 * TB :],
            ]
        )

    arrived = [lax.ppermute(leaving_tokens(j), ALL, to_groups(j)) for j in range(PIECES)]

    first_half = gather_x(first_both)
    ffn_both = with_partner(
        jnp.concatenate(
            [mine(gate_up_weight.reshape(shard, 2 * ffn)), mine(down_weight.T)], axis=1
        )
    )
    other_segments = core_flip(segments)

    col_at = jnp.arange(D, dtype=jnp.int32)
    block = col_at // half
    features = (
        ((zh ^ (block % 2)) * 4 + (block // 2) % 4) * shard
        + (core ^ (block // 8)) * half + col_at % half
    )[None, :]
    spots = jnp.arange(PIECES, dtype=jnp.int32) ^ y
    rows_x = (spots // 2) * 4 + 2 * (spots % 2)
    bases = jnp.concatenate(
        [(rows_x + side) * shard, (rows_x + 1 - side) * shard, y[None].astype(jnp.int32)]
    )
    source_low, normed, cot_mine, gains, inverse_first = arrange(bases, features, arrived)
    gain_first, gain_second = gains[0:1], gains[1:2]
    first_half, ffn_both, other_segments, normed = tie(
        first_half, ffn_both, other_segments, normed
    )

    first_other = core_flip(first_half)
    w_proj = jnp.concatenate([first_half, first_other], axis=0)
    out_half = first_half[:, proj_cols:]
    out_others = [y_flip(out_half, d) for d in range(1, 4)]
    projected = dot(normed[:, : D // 2], first_half) + dot(normed[:, D // 2 :], first_other)
    qkv = projected[:, : 3 * width].astype(BF)
    lanes = lax.broadcasted_iota(jnp.int32, (1, EXT), 1)
    earlier = (
        lax.broadcasted_iota(jnp.int32, (TB, TB), 0) >= lax.broadcasted_iota(jnp.int32, (TB, TB), 1)
    ).astype(F32)
    bias_lanes = jnp.pad(jnp.concatenate([forget_bias] * 3), (0, EXT - 3 * heads))[None, :]
    gate_logit = projected[:, 3 * width : 4 * width]
    forget_lanes = projected[:, 4 * width : proj_cols] + bias_lanes
    cumulative = jnp.dot(earlier, jax.nn.log_sigmoid(forget_lanes), precision=HIGHEST)
    rest = cumulative - rounded(cumulative)
    parts = jnp.where(
        lanes < heads, cumulative, jnp.where(lanes < 2 * heads, rest, rest - rounded(rest))
    ).astype(BF)

    sequence_block = 2 * core + x % 2
    key_values = jnp.concatenate([qkv[:, width:], parts], axis=1)
    halo1 = block_shift(key_values, 1)
    halo2 = block_shift(key_values, 2)
    cot_leaving = after(cot_mine, key_values)
    cot_others = [y_flip(cot_leaving, d) for d in range(1, 4)]
    own = jnp.where(x // 2 == core, segments, other_segments)
    own = lax.dynamic_index_in_dim(own, zh, 0, keepdims=False)
    padded = jnp.concatenate([jnp.full((2 * TB,), -1, jnp.int32), own])
    seg_k = lax.dynamic_slice_in_dim(padded, sequence_block * TB, KW)
    seg_q = lax.dynamic_slice_in_dim(own, sequence_block * TB, TB)[:, None]
    seg_k = seg_k[None, :]
    out_half = jnp.concatenate([out_half] + out_others, axis=1)
    halo1, halo2, qkv, gate_logit, seg_q, seg_k, out_half = tie(
        halo1, halo2, qkv, gate_logit, seg_q, seg_k, out_half
    )
    out_other = core_flip(out_half)
    ffn_half = gather_x(after(ffn_both, halo1))
    column = lax.broadcasted_iota(jnp.int32, (EXT, 8), 1)
    lane_at = lax.broadcasted_iota(jnp.int32, (EXT, 8), 0)
    gather_parts = ((lane_at % heads == column) & (lane_at < 3 * heads)).astype(BF)
    decay = lax.dot_general(
        gather_parts,
        jnp.concatenate([halo2[:, 2 * width :], halo1[:, 2 * width :], parts], axis=0),
        (((0,), (1,)), ((), ())),
        preferred_element_type=F32,
    )
    last1 = decay[:, 2 * TB - 1 : 2 * TB]
    last2 = decay[:, TB - 1 : TB] + last1
    key_at = lax.broadcasted_iota(jnp.int32, (1, KW), 1)
    decay = decay - jnp.where(key_at < TB, last2, jnp.where(key_at < 2 * TB, last1, 0.0))
    attended, gated, norm = attend(qkv, halo1, halo2, gate_logit, decay, seg_q, seg_k)
    gated, out_other, *cot_others = tie(gated, out_other, *cot_others)
    gated_others = [y_flip(gated, d) for d in range(1, 4)]
    w_out = tie(jnp.concatenate([out_half, out_other], axis=0))[0]
    ffn_half = after(ffn_half, *gated_others)
    w_ffn = jnp.concatenate([ffn_half, core_flip(ffn_half)], axis=0)
    w_gate_up, w_down = w_ffn[:, : 2 * ffn], w_ffn[:, 2 * ffn :]
    cot = jnp.concatenate(reorder(jnp.stack([cot_mine] + cot_others), y), axis=0)

    gated_all = jnp.concatenate([gated] + gated_others, axis=1)
    residual = source_low.astype(F32) + dot_t(gated_all, w_out)
    inverse_second = lax.rsqrt(jnp.mean(residual * residual, axis=1, keepdims=True) + EPS)
    normed_second = (residual * inverse_second * gain_second).astype(BF)
    gate_up = dot(normed_second, w_gate_up)
    gate_rows, up_rows = gate_up[:, :ffn], gate_up[:, ffn:]
    ffn_open = jax.nn.sigmoid(gate_rows)
    hidden = (gate_rows * ffn_open * up_rows).astype(BF)
    grad_hidden = dot(cot, w_down)
    grad_gate_up = jnp.concatenate(
        [
            (grad_hidden * up_rows * ffn_open * (1.0 + gate_rows * (1.0 - ffn_open))).astype(BF),
            (grad_hidden * gate_rows * ffn_open).astype(BF),
        ],
        axis=1,
    )

    def rows_of(matrix, index):
        return lax.dynamic_slice_in_dim(matrix, index * QUARTER, QUARTER, 0)

    def others_rows(partial):
        return [y_flip(rows_of(partial, y ^ d).astype(BF), d) for d in range(1, 4)]

    def summed(first, others):
        return first + sum(other.astype(F32) for other in others)

    partial_second = dot_t(grad_gate_up, w_gate_up)
    second_others = others_rows(partial_second)
    second_mine = rows_of(partial_second, y)

    gate_up_arrived = core_flip(leaving_rows(normed_second, grad_gate_up))
    down_arrived = core_flip(leaving_rows(cot, hidden))
    gate_up_mine = summed_rows(normed_second, grad_gate_up, gate_up_arrived)
    down_mine = summed_rows(cot, hidden, down_arrived)
    ffn_mine, *second_others = tie(
        jnp.concatenate([gate_up_mine, down_mine], axis=1), *second_others
    )
    ffn_scattered = scatter_x(ffn_mine)
    output_partial = dot_t(hidden, w_down)
    output_mine = rows_of(output_partial, y)
    output_leaving = [rows_of(output_partial, y ^ d).astype(BF) for d in range(1, 4)]
    second_others[0], output_mine, *output_leaving = tie(
        second_others[0], output_mine, *output_leaving
    )
    grad_normed_second = summed(second_mine, second_others)
    residual_mine = rows_of(residual, y)
    inverse_mine = rows_of(inverse_second, y)
    scaled = gain_second * grad_normed_second
    second_dot = jnp.sum(scaled * residual_mine, axis=1, keepdims=True)
    grad_residual = (
        cot_mine.astype(F32)
        + inverse_mine * scaled
        - residual_mine * (inverse_mine**3 * second_dot / D)
    )
    grad_branch = grad_residual.astype(BF)
    grad_gated_all = dot(grad_branch, w_out).astype(BF)
    gated_pieces = jnp.stack(
        [grad_gated_all[:, :width]]
        + [y_flip(grad_gated_all[:, d * width : (d + 1) * width], d) for d in range(1, 4)]
    )
    grad_gated = jnp.concatenate(reorder(gated_pieces, y), axis=0).astype(F32)
    grad_gated, grad_branch = tie(grad_gated, grad_branch)
    branch_others = [y_flip(grad_branch, d) for d in range(1, 4)]

    gate_open = jax.nn.sigmoid(gate_logit)
    grad_attended = (grad_gated * gate_open).astype(BF)
    dgate = (grad_gated * attended * gate_open * (1.0 - gate_open)).astype(BF)
    dq, dk, dv, d1, d2, forget_part = attend_back(
        qkv, halo1, halo2, grad_attended, decay, seg_q, seg_k, norm
    )
    d1, d2, dgate, ffn_scattered, *others = tie(
        d1, d2, dgate, ffn_scattered, *output_leaving, *branch_others
    )
    output_leaving, branch_others = others[:3], others[3:]
    back1 = block_shift(d1, -1)
    back2 = block_shift(d2, -2)
    output_others = [y_flip(output_leaving[d - 1], d) for d in range(1, 4)]

    grad_branch, dgate, dq, *branch_others = tie(grad_branch, dgate, dq, *branch_others, back2)[:-1]
    partial_early = dot_t(dq, w_proj[:, :width]) + dot_t(dgate, w_proj[:, 3 * width : 4 * width])
    branch_rows = jnp.concatenate([grad_branch] + branch_others, axis=0)
    gated_rows = jnp.concatenate([rows_of(gated, y ^ d) for d in range(4)], axis=0)
    sooner = jnp.concatenate([dgate, dq], axis=1)
    sooner_leaving = jnp.concatenate(
        [leaving_rows(branch_rows, gated_rows), leaving_rows(normed, sooner)], axis=1
    )
    ffn_near = near_sum(after(ffn_scattered, back2))
    back1, back2, ffn_near, sooner_leaving, *output_others = tie(
        back1, back2, ffn_near, sooner_leaving, *output_others
    )
    ffn_part = twin_sum(ffn_near)
    back1, back2 = back1.astype(F32), back2.astype(F32)
    key_sums = back1[:, : 2 * width] + back2[:, : 2 * width]
    output_mine = (residual_mine + summed(output_mine, output_others)).astype(BF)

    from_lane = lax.broadcasted_iota(jnp.int32, (EXT, 1), 0)
    same_head = (from_lane % heads == lanes % heads) & (lanes < 2 * heads)
    join = (same_head & (from_lane < 2 * heads)).astype(F32)
    join_far = (same_head & (from_lane >= 2 * heads) & (from_lane < 4 * heads)).astype(F32)
    sums1, sums2 = back1[:, 2 * width :], back2[:, 2 * width :]
    other_sums = jnp.dot(sums1 + sums2, join, precision=HIGHEST)
    later = jnp.sum(other_sums, axis=0, keepdims=True) + jnp.dot(
        sums1[:1], join_far, precision=HIGHEST
    )
    suffix = lax.dot_general(
        earlier, forget_part - other_sums, (((0,), (0,)), ((), ())), precision=HIGHEST
    ) + later
    grad_forget = suffix * jax.nn.sigmoid(-forget_lanes)
    grad_extra = jnp.where(
        lanes < heads, grad_forget, jnp.where(lanes < 2 * heads, grad_forget - rounded(grad_forget), 0.0)
    ).astype(BF)
    dk_all = (dk + key_sums[:, :width]).astype(BF)
    dv_all = (dv + key_sums[:, width:]).astype(BF)

    late = jnp.concatenate([dk_all, dv_all, grad_extra], axis=1)
    leaving_late = leaving_rows(normed, late)
    attn_arrived = core_flip(by_rows(jnp.concatenate([sooner_leaving, leaving_late], axis=1)))
    early_cols = 3 * width
    attn_mine = jnp.concatenate(
        [
            summed_rows(branch_rows, gated_rows, attn_arrived[:, :width]),
            summed_rows(normed, sooner, attn_arrived[:, width:early_cols]),
            summed_rows(normed, late, attn_arrived[:, early_cols:]),
        ],
        axis=1,
    )
    attn_mine = by_rows(attn_mine)
    attn_scattered = scatter_x(attn_mine)
    late = after(late, attn_mine)
    partial_first = (
        partial_early
        + dot_t(late[:, : 2 * width], w_proj[:, width : 3 * width])
        + dot_t(late[:, 2 * width :], w_proj[:, 4 * width : proj_cols])
    )

    leaving = release(
        bases, features, partial_first, source_low, inverse_first, gain_first, grad_residual, output_mine
    )
    ffn_other = core_flip(rounded(ffn_part).astype(BF))
    leaving, ffn_part = tie(leaving, ffn_part)
    returned = [lax.ppermute(leaving[j], ALL, from_groups(j)) for j in range(PIECES)]
    bias_sum = after(
        jnp.broadcast_to(jnp.sum(grad_forget, axis=0, keepdims=True), (8, EXT)), leaving
    )
    for other in (core_flip, lambda v: x_flip(v, 1), lambda v: x_flip(v, 2), z_partner, z_twin):
        bias_sum = bias_sum + other(bias_sum)
    attn_part = twin_sum(near_sum(attn_scattered))
    bias_sum, *returned = tie(bias_sum, *returned)
    input_rows = sum(piece[:TB].astype(F32) for piece in returned)
    output_rows = jnp.concatenate(reorder(jnp.stack([piece[TB:] for piece in returned]), spot), axis=0)
    far_rows = x_flip(
        jnp.concatenate([input_rows[:, shard:].astype(BF), output_rows[:, shard:]], axis=0), 1
    )
    near, far = input_rows[:, :shard], far_rows[:TB].astype(F32)
    input_grad = jnp.concatenate(
        [jnp.where(side == 0, near, far), jnp.where(side == 0, far, near)], axis=0
    )
    near, far = output_rows[:, :shard], far_rows[TB:]
    block_output = jnp.concatenate(
        [jnp.where(side == 0, near, far), jnp.where(side == 0, far, near)], axis=0
    )

    ffn_full = both_halves(ffn_part, ffn_other, core)
    attn_other = core_flip(rounded(attn_part).astype(BF))
    attn_all = both_halves(attn_part, attn_other, core)
    attn_part = after(attn_part, attn_other)
    extras = attn_all[:, 5 * width :]
    forget_grad = extras[:, :heads] + extras[:, heads : 2 * heads]
    attn_full = jnp.concatenate(
        [attn_all[:, 2 * width : 5 * width], attn_all[:, width : 2 * width]], axis=1
    )

    def row_dot(weight, grad):
        return jnp.sum(mine(weight).astype(F32) * grad, axis=1)

    gain_parts = jnp.stack(
        [
            (
                row_dot(attn_weight[:, :3].reshape(shard, 3 * width), attn_part[:, 2 * width : 5 * width])
                + row_dot(attn_weight[:, 3], attn_part[:, width : 2 * width])
                + row_dot(
                    jnp.concatenate([forget_weight] * 2, axis=1),
                    attn_part[:, 5 * width : 5 * width + 2 * heads],
                )
            )
            / mine(attn_gain).astype(F32),
            row_dot(gate_up_weight.reshape(shard, 2 * ffn), ffn_part[:, : 2 * ffn])
            / mine(ffn_gain).astype(F32),
        ]
    )
    gain_others = [y_flip(gain_parts, d) for d in range(1, 4)]
    gain_half = (gain_parts + gain_others[0]) + (gain_others[1] + gain_others[2])
    gain_other = core_flip(gain_half)
    gain_sum = jnp.where(
        core == 0,
        jnp.concatenate([gain_half, gain_other], axis=1),
        jnp.concatenate([gain_other, gain_half], axis=1),
    )
    return (
        block_output,
        input_grad,
        gain_sum[0],
        attn_full.reshape(attn_weight.shape),
        forget_grad,
        bias_sum[0, :heads],
        attn_all[:, :width].T,
        gain_sum[1],
        ffn_full[:, : 2 * ffn].reshape(gate_up_weight.shape),
        ffn_full[:, 2 * ffn :].T,
    )


def solution(mesh):
    inner = Mesh(mesh.devices.reshape(DIMS), ALL)
    dp, row = ("zl", "core"), ("zh", "x")
    tokens = P(("zl", "core", "y"), row)
    in_specs = (
        tokens, P(row), P(row, None, "y"), P(row, "y"), P("y"), P("y", row), P(row),
        P(row, None, "y"), P("y", row), P(dp, None), tokens,
    )
    out_specs = (
        tokens, tokens, P(row), P(row, None, "y"), P(row, "y"), P("y"), P("y", row), P(row),
        P(row, None, "y"), P("y", row),
    )
    return jax.shard_map(body, mesh=inner, in_specs=in_specs, out_specs=out_specs, check_vma=False)
```
